256 devices in a mesh: ctx: 64 (over x, z_lo, y), chan: 4 (over z_hi, core).
Axes of the slice: x: 4, y: 4, z: 8 (z_hi: 2, z_lo: 4; z = z_hi * 4 + z_lo), core: 2. Of those that a mesh axis runs over, the one named last changes fastest.
Arguments:
- token_ids: int32 [16384], P('ctx'), may hold values from 0 to 511
- domain_ids: int32 [16384], P('ctx'), may hold values from 0 to 7
- domain_counts: int32 [64, 8], P('ctx'), may hold values from 16 to 141, as said below
- embed_table: bfloat16 [512, 4096], P(None, 'chan'), may hold values from -6 to 6
- query_act: bfloat16 [4096, 16384], P('chan', 'ctx'), may hold values from -6 to 6
- key_act: bfloat16 [4096, 16384], P('chan', 'ctx'), may hold values from -6 to 6
- conv_saved: bfloat16 [4096, 16384], P('chan', 'ctx'), may hold values from -6 to 6
- loss_seed: bfloat16 [4096, 16384], P('chan', 'ctx'), may hold values from -6 to 6
- filters: float32 [4096, 16384], P('chan', 'ctx')
- skip_gain: float32 [4096], P('chan'), may hold values from 0.5 to 1.5
Outputs:
- grad_query: float32 [4096, 16384], P('chan', 'ctx')
- grad_key: float32 [4096, 16384], P('chan', 'ctx')
- grad_value: float32 [4096, 16384], P('chan', 'ctx')
- grad_filter: float32 [4096, 16384], P('chan', 'ctx')
The draws below stay inside these ranges and needn't reach their ends.
Inputs may be any that keep to these rules, and one draw needn't show every extreme that they name: `domain_counts`: each entry is a positive token count.
All inputs are finite; a program needn't handle non-finite values.
Results may differ from the reference program's by a relative error of at most 0.0028.
Values sent between devices are 32-bit elements; how exact they have to be, the bound alone decides.
A program may use at most 128 MiB of HBM per device.

```python
import math
import jax
import jax.numpy as jnp
import numpy as np
from jax import lax

C = 4096
VOCAB = 512
NDOM = 8
TOKENS = 16384
N_CTX = 64


def draw_domain_counts(key, part):
    key = jax.random.fold_in(key, 7)
    base = jax.random.randint(key, (N_CTX, NDOM), 16, 48)
    base = base.at[0, 0].set(16).at[N_CTX - 1, 0].set(47)
    rising = N_CTX - 1 + 2 * jnp.arange(N_CTX, dtype=jnp.int32)[:, None]
    return base * rising // (N_CTX - 1)


def draw_filters(key, part):
    key = jax.random.fold_in(key, 11)
    first, second = jax.random.split(key)
    lower, upper = (math.log(40.0), math.log(TOKENS * 4.0))
    reach = jnp.exp(jax.random.uniform(first, (C, 1), jnp.float32, lower, upper))
    places = jnp.arange(TOKENS, dtype=jnp.float32)[None, :]
    height = jnp.sqrt((1.0 - jnp.exp(-2.0 / reach)) / (1.0 - jnp.exp(-2.0 * TOKENS / reach)))
    noise = jax.random.normal(second, (C, TOKENS), jnp.float32)
    return noise * height * jnp.exp(-places / reach)


def set_ends(drawn, own_key, least, high):
    shape = drawn.shape
    spot = [jax.random.randint(jax.random.fold_in(own_key, axis), (), 0, shape[axis]) for axis in range(len(shape))]
    drawn = drawn.at[tuple(spot)].set(least)
    longest = shape.index(max(shape))
    spot[longest] = (spot[longest] + 1) % shape[longest]
    return drawn.at[tuple(spot)].set(high)


def level_of(own_key, shape, shards, least, largest):
    gain = 1.0
    for dim, parts in shards:
        draws = jax.random.uniform(jax.random.fold_in(jax.random.fold_in(own_key, 6), dim), (parts,), jnp.float32, least / len(shards), largest / len(shards))
        gain = gain * jnp.repeat(jnp.exp(draws), shape[dim] // parts).reshape((-1,) + (1,) * (len(shape) - 1 - dim))
    return gain


def cumulative_ranks(number_of, slope):
    portions = [(1 << 20) // math.isqrt(rank ** slope) + 1 for rank in range(1, number_of + 1)]
    spread = 1 + sum(portions) // (1 << 30)
    return np.cumsum(np.array([max(1, weight // spread) for weight in portions]))


def ranked(own_key, shape, count, skew):
    grid = cumulative_ranks(count, skew)
    ticket = jax.random.randint(jax.random.fold_in(own_key, 1), shape, 0, int(grid[count - 1]))
    rank = jnp.searchsorted(jnp.asarray(grid, jnp.int32), ticket, side="right")
    return jax.random.permutation(jax.random.fold_in(own_key, 2), count)[rank].astype(jnp.int32)


def gaussian(rng, dims, width, most, cuts=(), held_as=jnp.bfloat16):
    array = width * jax.random.normal(rng, dims, jnp.float32)
    if cuts:
        array = array * level_of(rng, dims, cuts, -0.22, 0.18)
    return jnp.clip(array, -most, most).astype(held_as)


def setup_inputs(seed: int = 0) -> dict:
    key_list = jax.random.split(jax.random.key(seed), 11)
    token_ids = set_ends(ranked(key_list[0], (TOKENS,), VOCAB, 2), jax.random.fold_in(key_list[0], 3), 0, VOCAB - 1).astype(jnp.int32)
    domain_ids = set_ends(jax.random.randint(key_list[1], (TOKENS,), 0, NDOM), jax.random.fold_in(key_list[1], 1), 0, NDOM - 1).astype(jnp.int32)
    domain_counts = draw_domain_counts(jax.random.fold_in(key_list[10], 71), 0)
    embed_table = gaussian(key_list[3], (VOCAB, C), 1.0, 6.0, ((1, 4),))
    query_act = gaussian(key_list[4], (C, TOKENS), 1.0, 6.0, ((0, 4), (1, 64)))
    key_act = gaussian(key_list[5], (C, TOKENS), 1.0, 6.0, ((0, 4), (1, 64)))
    conv_saved = gaussian(key_list[6], (C, TOKENS), 1.0, 6.0, ((0, 4), (1, 64)))
    loss_seed = gaussian(key_list[7], (C, TOKENS), 1.0, 6.0, ((0, 4), (1, 64)))
    filters = draw_filters(jax.random.fold_in(key_list[10], 71), 0)
    skip_gain = jnp.clip(0.5 + 1.0 * jax.random.uniform(key_list[9], (C,), jnp.float32) ** level_of(key_list[9], (C,), ((0, 4),), -0.2, 0.2), 0.5, 1.5)
    return dict(token_ids=token_ids, domain_ids=domain_ids, domain_counts=domain_counts, embed_table=embed_table, query_act=query_act, key_act=key_act, conv_saved=conv_saved, loss_seed=loss_seed, filters=filters, skip_gain=skip_gain)


count_unit = 64.0


def reference(token_ids, domain_ids, domain_counts, embed_table, query_act, key_act, conv_saved, loss_seed, filters, skip_gain):
    values = jnp.take(embed_table, token_ids, axis=0).T.astype(jnp.float32)
    keyed = key_act.astype(jnp.float32)
    mixed = keyed * values
    totals = jnp.sum(domain_counts.astype(jnp.float32), axis=0)
    weight = (count_unit * N_CTX) / totals[domain_ids]
    rounded = (loss_seed.astype(jnp.float32) * weight[None, :]).astype(jnp.bfloat16)
    upstream = lax.optimization_barrier(rounded).astype(jnp.float32)
    grad_query = upstream * conv_saved.astype(jnp.float32)
    dconv = upstream * query_act.astype(jnp.float32)
    length = 2 * TOKENS
    block = math.gcd(C, 256)

    def one_block(pieces):
        mix_b, filt_b, dconv_b = pieces
        spec_z = jnp.fft.rfft(mix_b, n=length, axis=1)
        spec_h = jnp.fft.rfft(filt_b, n=length, axis=1)
        spec_s = jnp.fft.rfft(dconv_b, n=length, axis=1)
        corr = jnp.fft.irfft(jnp.conj(spec_h) * spec_s, n=length, axis=1)[:, :TOKENS]
        fgrad = jnp.fft.irfft(jnp.conj(spec_z) * spec_s, n=length, axis=1)[:, :TOKENS]
        return corr, fgrad

    shaped = (mixed.reshape(C // block, block, TOKENS), filters.reshape(C // block, block, TOKENS), dconv.reshape(C // block, block, TOKENS))
    corr, fgrad = lax.map(one_block, shaped)
    corr = corr.reshape(C, TOKENS).astype(jnp.float32)
    fgrad = fgrad.reshape(C, TOKENS).astype(jnp.float32)
    back = corr + skip_gain[:, None] * dconv
    grad_filter = fgrad * (TOKENS ** -0.5)
    return grad_query, back * values, back * keyed, grad_filter
```

```python
import functools

import jax
import jax.numpy as jnp
import ml_dtypes
import numpy as np
from jax import lax
from jax.experimental import pallas as pl
from jax.experimental.pallas import tpu as pltpu
from jax.sharding import PartitionSpec as P

MESH = pl.DeviceIdType.MESH
F32, BF16 = jnp.float32, jnp.bfloat16
count_unit = 64.0
LANES = 128
GROUP = 8
CHUNKS = 2


def split_host(x):
    high = x.astype(np.float32).astype(ml_dtypes.bfloat16)
    low = (x - high.astype(np.float64)).astype(np.float32).astype(ml_dtypes.bfloat16)
    return high, low


def constants(parts, width):
    total = parts * width
    j, r = np.arange(parts), np.arange(width)
    theta = 2.0 * np.pi * np.outer(j + 0.25, j) / parts
    first = np.concatenate([np.cos(theta), -np.sin(theta)], 0)
    phase = 2.0 * np.pi * np.outer(j + 0.25, r) / total
    turn = np.stack([np.cos(phase), np.sin(phase)]).astype(np.float32)
    omega = 2.0 * np.pi * (np.outer(r, r) % width) / width
    cosine, sine = np.cos(omega), np.sin(omega)
    inner = np.block([[cosine, -sine], [sine, cosine]])
    last = np.concatenate([np.cos(theta).T, np.sin(theta).T], 1) / total
    fh, fl = split_host(first)
    lh, ll = split_host(last)
    first_cat = np.concatenate([fh, fh, fl], 1)
    last_cat = np.concatenate([lh, lh, ll], 1)
    return first_cat, np.stack(split_host(inner)), last_cat, turn


def split(x):
    high = x.astype(BF16)
    return high, (x - high.astype(F32)).astype(BF16)


def dot(a, b):
    return jnp.dot(a, b, preferred_element_type=F32)


def turned(a, b, cosine, sine):
    return a * cosine + b * sine, b * cosine - a * sine


def kernel(
    parts, width,
    counts, tokens, domains, skip, first, last, turn,
    embed, query, key, loss, filters, inner,
    out, values_out, weight_out,
    cnt_src, cnt_all, embed_v, query_v, key_v, loss_v, inner_v, values_v,
    md, rf, rfh, rmd, res,
    load_sem, keep_sem, send_sem, recv_sem,
):
    me = lax.axis_index("ctx")
    chan = lax.axis_index("chan")
    rows = CHUNKS * GROUP
    halves = width // LANES
    tall = rows * halves
    barrier = pltpu.get_barrier_semaphore()

    def greet(k, carry):
        peer = lax.rem(me + k, parts)
        pl.semaphore_signal(barrier, inc=1, device_id=(peer, chan), device_id_type=MESH)
        return carry

    lax.fori_loop(1, parts, greet, 0)

    loads = [
        pltpu.make_async_copy(source, target, load_sem.at[i])
        for i, (source, target) in enumerate(
            [(embed, embed_v), (key, key_v), (query, query_v), (loss, loss_v), (inner, inner_v)]
        )
    ]
    for load in loads:
        load.start()
    cnt_src[...] = jnp.zeros_like(cnt_src)
    cnt_src[0:1, 0 : counts.shape[1]] = counts[...].astype(F32)

    def rows_of(ref, index):
        size = ref.shape[0] // parts
        return ref.at[pl.ds(pl.multiple_of(index * size, size), size)]

    def send(source, target, slot):
        own = pltpu.make_async_copy(rows_of(source, me), rows_of(target, me), recv_sem.at[slot])
        own.start()

        def go(k, carry):
            peer = lax.rem(me + k, parts)
            pltpu.make_async_remote_copy(
                src_ref=rows_of(source, peer),
                dst_ref=rows_of(target, me),
                send_sem=send_sem.at[slot],
                recv_sem=recv_sem.at[slot],
                device_id=(peer, chan),
                device_id_type=MESH,
            ).start()
            return carry

        lax.fori_loop(1, parts, go, 0)

    def arrived(target, slot):
        pltpu.make_async_copy(target, target, recv_sem.at[slot]).wait()

    def sent(target, slot):
        done = target.at[pl.ds(0, target.shape[0] // parts * (parts - 1))]
        pltpu.make_async_copy(done, done, send_sem.at[slot]).wait()

    pl.semaphore_wait(barrier, parts - 1)

    own = pltpu.make_async_copy(cnt_src, cnt_all.at[me], recv_sem.at[0])
    own.start()

    def tell(k, carry):
        peer = lax.rem(me + k, parts)
        pltpu.make_async_remote_copy(
            src_ref=cnt_src,
            dst_ref=cnt_all.at[me],
            send_sem=send_sem.at[0],
            recv_sem=recv_sem.at[0],
            device_id=(peer, chan),
            device_id_type=MESH,
        ).start()
        return carry

    lax.fori_loop(1, parts, tell, 0)
    send(filters, rf, 1)

    loads[0].wait()
    vocab = embed_v.shape[0]
    onehot = (
        lax.broadcasted_iota(jnp.int32, (vocab, width), 0) == tokens[...]
    ).astype(F32).astype(BF16)
    piece = 128

    def look_up(b, carry):
        at = pl.multiple_of(b * piece, piece)
        values_v[pl.ds(at, piece), :] = lax.dot_general(
            embed_v[:, pl.ds(at, piece)], onehot, (((0,), (0,)), ((), ())),
            preferred_element_type=F32,
        )
        return carry

    lax.fori_loop(0, values_v.shape[0] // piece, look_up, 0)
    keep = pltpu.make_async_copy(values_v, values_out, keep_sem)
    keep.start()
    for load in loads[1:4]:
        load.wait()
    arrived(cnt_all, 0)
    totals = jnp.sum(cnt_all[...], axis=0)[0:1, :]
    shares = (count_unit * parts) / totals
    weight = jnp.zeros((1, width), F32)
    for d in range(counts.shape[1]):
        weight = jnp.where(domains[...] == d, shares[0:1, d : d + 1], weight)
    weight_out[...] = weight

    def products(b, carry):
        at = pl.multiple_of(b * piece, piece)
        block = pl.ds(at, piece)
        mixed = key_v[block, :].astype(F32) * values_v[block, :]
        upstream = (loss_v[block, :].astype(F32) * weight).astype(BF16).astype(F32)
        dconv = upstream * query_v[block, :].astype(F32)
        for q in range(piece // rows):
            for chunk in range(CHUNKS):
                part = slice(q * rows + chunk * GROUP, q * rows + (chunk + 1) * GROUP)
                for h in range(halves):
                    start = pl.multiple_of((at + q * rows) * halves + h * GROUP, GROUP)
                    lanes = slice(h * LANES, (h + 1) * LANES)
                    md[chunk, pl.ds(start, GROUP), :] = mixed[part, lanes]
                    start = start + halves * GROUP
                    md[chunk, pl.ds(start, GROUP), :] = dconv[part, lanes]
        return carry

    lax.fori_loop(0, values_v.shape[0] // piece, products, 0)
    for chunk in range(CHUNKS):
        send(md.at[chunk], rmd.at[chunk], 2 + chunk)

    loads[4].wait()
    arrived(rf, 1)

    def halve(b, carry):
        at = pl.multiple_of(b * piece, piece)
        block = rf[pl.ds(at, piece), :]
        for q in range(piece // GROUP):
            for h in range(halves):
                start = pl.multiple_of((at + q * GROUP) * halves + h * GROUP, GROUP)
                rfh[pl.ds(start, GROUP), :] = block[
                    q * GROUP : (q + 1) * GROUP, h * LANES : (h + 1) * LANES
                ]
        return carry

    lax.fori_loop(0, rf.shape[0] // piece, halve, 0)

    def column(ref, start):
        return jnp.concatenate(
            [ref[pl.ds(start + h * GROUP, parts, stride=tall), :] for h in range(halves)], axis=1
        )

    def inner_transform(real, imag):
        high, low = split(jnp.concatenate([real, imag], axis=1))
        return dot(high, inner_v[0]) + dot(low, inner_v[0]) + dot(high, inner_v[1])

    def channel(chunk, c, carry):
        cosine, sine = turn[0], turn[1]
        signals = [
            column(rfh, chunk * GROUP * halves + c),
            column(rmd.at[chunk], c),
            column(rmd.at[chunk], GROUP * halves + c),
        ]
        high, low = split(jnp.concatenate(signals, axis=1))
        spread = dot(first[...], jnp.concatenate([high, low, high], axis=0))
        pairs = [
            turned(
                spread[:parts, s * width : (s + 1) * width],
                spread[parts:, s * width : (s + 1) * width],
                cosine, sine,
            )
            for s in range(3)
        ]
        spectra = inner_transform(
            jnp.concatenate([p[0] for p in pairs], axis=0),
            jnp.concatenate([p[1] for p in pairs], axis=0),
        )
        real, imag = spectra[:, :width], spectra[:, width:]
        sr, si = real[2 * parts :], imag[2 * parts :]
        both_r = [real[s * parts : (s + 1) * parts] * sr + imag[s * parts : (s + 1) * parts] * si for s in (0, 1)]
        both_i = [imag[s * parts : (s + 1) * parts] * sr - real[s * parts : (s + 1) * parts] * si for s in (0, 1)]
        back = inner_transform(jnp.concatenate(both_r, axis=0), jnp.concatenate(both_i, axis=0))
        pairs = [
            turned(back[s * parts : (s + 1) * parts, :width], back[s * parts : (s + 1) * parts, width:], cosine, sine)
            for s in (0, 1)
        ]
        folded = jnp.concatenate(
            [jnp.concatenate([p[0] for p in pairs], axis=1), jnp.concatenate([p[1] for p in pairs], axis=1)],
            axis=0,
        )
        high, low = split(folded)
        result = dot(last[...], jnp.concatenate([high, low, high], axis=0))
        gain = skip[me * rows + chunk * GROUP + c]
        both = (
            result[:, :width] + gain * signals[2],
            result[:, width:] * ((parts * width) ** -0.5),
        )
        for s in range(2):
            for h in range(halves):
                start = (s * halves + h) * GROUP + c
                res[chunk, pl.ds(start, parts, stride=tall), :] = both[s][
                    :, h * LANES : (h + 1) * LANES
                ]
        return carry

    for chunk in range(CHUNKS):
        arrived(rmd.at[chunk], 2 + chunk)
        lax.fori_loop(0, GROUP, functools.partial(channel, chunk), 0)
        send(res.at[chunk], out.at[chunk], 4 + chunk)

    keep.wait()
    done = cnt_all.at[pl.ds(0, parts - 1)]
    pltpu.make_async_copy(done, done, send_sem.at[0]).wait()
    sent(rf, 1)
    for chunk in range(CHUNKS):
        sent(rmd.at[chunk], 2 + chunk)
    for chunk in range(CHUNKS):
        sent(res.at[chunk], 4 + chunk)
        arrived(out.at[chunk], 4 + chunk)


def on_device(
    token_ids, domain_ids, domain_counts, embed_table, query_act, key_act, conv_saved,
    loss_seed, filters, skip_gain,
):
    parts = lax.axis_size("ctx")
    chans, width = query_act.shape
    vocab = embed_table.shape[0]
    first, inner, last, turn = [jnp.asarray(x) for x in constants(parts, width)]
    vmem = pl.BlockSpec(memory_space=pltpu.VMEM)
    smem = pl.BlockSpec(memory_space=pltpu.SMEM)
    hbm = pl.BlockSpec(memory_space=pl.ANY)
    rows = CHUNKS * GROUP
    halves = width // LANES
    assert chans == parts * rows
    out, values, weight = pl.pallas_call(
        functools.partial(kernel, parts, width),
        out_shape=(
            jax.ShapeDtypeStruct((CHUNKS, chans * halves, LANES), F32),
            jax.ShapeDtypeStruct((chans, width), F32),
            jax.ShapeDtypeStruct((1, width), F32),
        ),
        in_specs=[vmem, vmem, vmem, smem, vmem, vmem, vmem] + [hbm] * 6,
        out_specs=(hbm, hbm, vmem),
        scratch_shapes=[
            pltpu.VMEM((8, LANES), F32),
            pltpu.VMEM((parts, 8, LANES), F32),
            pltpu.VMEM((vocab, chans), BF16),
            pltpu.VMEM((chans, width), BF16),
            pltpu.VMEM((chans, width), BF16),
            pltpu.VMEM((chans, width), BF16),
            pltpu.VMEM(inner.shape, BF16),
            pltpu.VMEM((chans, width), F32),
            pltpu.VMEM((CHUNKS, chans * halves, LANES), F32),
            pltpu.VMEM((chans, width), F32),
            pltpu.VMEM((chans * halves, LANES), F32),
            pltpu.VMEM((CHUNKS, chans * halves, LANES), F32),
            pltpu.VMEM((CHUNKS, chans * halves, LANES), F32),
            pltpu.SemaphoreType.DMA((5,)),
            pltpu.SemaphoreType.DMA,
            pltpu.SemaphoreType.DMA((6,)),
            pltpu.SemaphoreType.DMA((6,)),
        ],
        compiler_params=pltpu.CompilerParams(
            collective_id=0, has_side_effects=True, vmem_limit_bytes=40 * 2**20
        ),
        name="exchange",
    )(
        domain_counts, token_ids[None, :], domain_ids[None, :], skip_gain, first, last, turn,
        embed_table, query_act, key_act, loss_seed, filters, inner,
    )
    sorted_out = out.reshape(CHUNKS, parts, 2, halves, GROUP, LANES).transpose(2, 1, 0, 4, 3, 5)
    back = sorted_out[0].reshape(chans, width)
    grad_filter = sorted_out[1].reshape(chans, width)
    rounded = (loss_seed.astype(F32) * weight).astype(BF16)
    upstream = lax.optimization_barrier(rounded).astype(F32)
    grad_query = upstream * conv_saved.astype(F32)
    return grad_query, back * values, back * key_act.astype(F32), grad_filter


def solution(mesh):
    in_specs = (
        P("ctx"), P("ctx"), P("ctx", None), P(None, "chan"),
        P("chan", "ctx"), P("chan", "ctx"), P("chan", "ctx"), P("chan", "ctx"), P("chan", "ctx"),
        P("chan"),
    )
    out_specs = (P("chan", "ctx"),) * 4
    return jax.shard_map(
        on_device, mesh=mesh, in_specs=in_specs, out_specs=out_specs, check_vma=False
    )
```

```python
import functools

import jax
import jax.numpy as jnp
import ml_dtypes
import numpy as np
from jax import lax
from jax.experimental import pallas as pl
from jax.experimental.pallas import tpu as pltpu
from jax.sharding import PartitionSpec as P

MESH = pl.DeviceIdType.MESH
F32, BF16 = jnp.float32, jnp.bfloat16
count_unit = 64.0
LANES = 128
GROUP = 8
CHUNKS = 2


def split_host(x):
    high = x.astype(np.float32).astype(ml_dtypes.bfloat16)
    low = (x - high.astype(np.float64)).astype(np.float32).astype(ml_dtypes.bfloat16)
    return high, low


def constants(parts, width):
    total = parts * width
    j, r = np.arange(parts), np.arange(width)
    theta = 2.0 * np.pi * np.outer(j + 0.25, j) / parts
    first = np.concatenate([np.cos(theta), -np.sin(theta)], 0)
    phase = 2.0 * np.pi * np.outer(j + 0.25, r) / total
    omega = 2.0 * np.pi * (np.outer(r, r) % width) / width
    cosine, sine = np.cos(omega), np.sin(omega)
    inner = np.block([[cosine, -sine], [sine, cosine]])
    last = np.concatenate([np.cos(theta).T, np.sin(theta).T], 1) / total
    fh, fl = split_host(first)
    lh, ll = split_host(last)
    first_cat = np.concatenate([fh, fh, fl], 1)
    last_cat = np.concatenate([lh, lh, ll], 1)
    table = np.zeros((2 * width + 4 * parts, 2 * width), np.float32)
    table[: 2 * width] = inner
    table[2 * width : 2 * width + parts] = np.concatenate([np.cos(phase), np.sin(phase)], 1)
    table[2 * width + parts : 2 * width + 3 * parts, : 3 * parts] = first_cat
    table[2 * width + 3 * parts :, : 6 * parts] = last_cat
    return table


def split(x):
    high = x.astype(BF16)
    return high, (x - high.astype(F32)).astype(BF16)


def dot(a, b):
    return jnp.dot(a, b, preferred_element_type=F32)


def turned(a, b, cosine, sine):
    return a * cosine + b * sine, b * cosine - a * sine


def kernel(
    parts, width,
    counts, tokens, domains, skip, table,
    embed, query, key, saved, loss, filters,
    grad_query, grad_key, grad_value, grad_filter,
    counts_v, tokens_v, domains_v, skip_s, table_v,
    cnt_src, cnt_all, embed_v, query_v, key_v, saved_v, loss_v, first, last, inner_v,
    values_v, keyed_v, out,
    md, rf, rfh, rmd, res_h, res,
    load_sem, send_sem, recv_sem,
):
    me = lax.axis_index("ctx")
    chan = lax.axis_index("chan")
    rows = CHUNKS * GROUP
    halves = width // LANES
    tall = rows * halves
    barrier = pltpu.get_barrier_semaphore()

    def greet(k, carry):
        peer = lax.rem(me + k, parts)
        pl.semaphore_signal(barrier, inc=1, device_id=(peer, chan), device_id_type=MESH)
        return carry

    lax.fori_loop(1, parts, greet, 0)

    loads = [
        pltpu.make_async_copy(source, target, load_sem.at[i])
        for i, (source, target) in enumerate(
            [
                (counts, counts_v), (tokens, tokens_v), (domains, domains_v), (embed, embed_v),
                (key, key_v), (query, query_v), (saved, saved_v), (loss, loss_v),
                (skip, skip_s), (table, table_v),
            ]
        )
    ]
    for load in loads:
        load.start()
    domain_count = counts.shape[1]
    cnt_src[...] = jnp.zeros_like(cnt_src)
    loads[0].wait()
    cnt_src[0:1, 0:domain_count] = counts_v[...].astype(F32)

    def rows_of(ref, index):
        size = ref.shape[0] // parts
        return ref.at[pl.ds(pl.multiple_of(index * size, size), size)]

    def send(source, target, slot):
        own = pltpu.make_async_copy(source(me), target(me), recv_sem.at[slot])
        own.start()

        def go(k, carry):
            peer = lax.rem(me + k, parts)
            pltpu.make_async_remote_copy(
                src_ref=source(peer),
                dst_ref=target(me),
                send_sem=send_sem.at[slot],
                recv_sem=recv_sem.at[slot],
                device_id=(peer, chan),
                device_id_type=MESH,
            ).start()
            return carry

        lax.fori_loop(1, parts, go, 0)

    def arrived(target, slot):
        pltpu.make_async_copy(target, target, recv_sem.at[slot]).wait()

    def sent(target, slot):
        done = target.at[pl.ds(0, target.shape[0] // parts * (parts - 1))]
        pltpu.make_async_copy(done, done, send_sem.at[slot]).wait()

    pl.semaphore_wait(barrier, parts - 1)

    pltpu.make_async_copy(cnt_src, cnt_all.at[me], recv_sem.at[0]).start()
    pltpu.make_async_copy(rows_of(filters, me), rows_of(rf, me), recv_sem.at[1]).start()

    def tell(k, carry):
        peer = lax.rem(me + k, parts)
        for slot, source, target in (
            (0, cnt_src, cnt_all.at[me]), (1, rows_of(filters, peer), rows_of(rf, me)),
        ):
            pltpu.make_async_remote_copy(
                src_ref=source,
                dst_ref=target,
                send_sem=send_sem.at[slot],
                recv_sem=recv_sem.at[slot],
                device_id=(peer, chan),
                device_id_type=MESH,
            ).start()
        return carry

    lax.fori_loop(1, parts, tell, 0)

    for load in loads[1:4]:
        load.wait()
    vocab = embed_v.shape[0]
    onehot = (
        lax.broadcasted_iota(jnp.int32, (vocab, width), 0) == tokens_v[...]
    ).astype(F32).astype(BF16)
    piece = 128

    def look_up(b, carry):
        at = pl.multiple_of(b * piece, piece)
        values_v[pl.ds(at, piece), :] = lax.dot_general(
            embed_v[:, pl.ds(at, piece)], onehot, (((0,), (0,)), ((), ())),
            preferred_element_type=F32,
        )
        return carry

    lax.fori_loop(0, values_v.shape[0] // piece, look_up, 0)
    for load in loads[4:8]:
        load.wait()
    arrived(cnt_all, 0)
    totals = jnp.sum(cnt_all[...], axis=0)
    shares = (count_unit * parts) / totals
    weight = jnp.zeros((1, width), F32)
    for d in range(domain_count):
        weight = jnp.where(domains_v[...] == d, shares[0:1, d : d + 1], weight)

    def products(b, carry):
        at = pl.multiple_of(b * piece, piece)
        block = pl.ds(at, piece)
        keyed = key_v[block, :].astype(F32)
        keyed_v[block, :] = keyed
        mixed = keyed * values_v[block, :]
        upstream = (loss_v[block, :].astype(F32) * weight).astype(BF16).astype(F32)
        grad_query[block, :] = upstream * saved_v[block, :].astype(F32)
        dconv = upstream * query_v[block, :].astype(F32)
        for q in range(piece // rows):
            for chunk in range(CHUNKS):
                part = slice(q * rows + chunk * GROUP, q * rows + (chunk + 1) * GROUP)
                for h in range(halves):
                    start = pl.multiple_of((at + q * rows) * halves + h * GROUP, GROUP)
                    lanes = slice(h * LANES, (h + 1) * LANES)
                    md[chunk, pl.ds(start, GROUP), :] = mixed[part, lanes]
                    start = start + halves * GROUP
                    md[chunk, pl.ds(start, GROUP), :] = dconv[part, lanes]
        return carry

    lax.fori_loop(0, values_v.shape[0] // piece, products, 0)
    for chunk in range(CHUNKS):
        send(
            lambda i: rows_of(md.at[chunk], i), lambda i: rows_of(rmd.at[chunk], i), 2 + chunk
        )

    for load in loads[8:]:
        load.wait()
    double = 2 * width
    first[...] = table_v[double + parts : double + 3 * parts, 0 : 3 * parts].astype(BF16)
    last[...] = table_v[double + 3 * parts : double + 4 * parts, 0 : 6 * parts].astype(BF16)
    inner_v[0], inner_v[1] = split(table_v[0:double, :])
    arrived(rf, 1)

    def halve(b, carry):
        at = pl.multiple_of(b * piece, piece)
        block = rf[pl.ds(at, piece), :]
        for q in range(piece // GROUP):
            for h in range(halves):
                start = pl.multiple_of((at + q * GROUP) * halves + h * GROUP, GROUP)
                rfh[pl.ds(start, GROUP), :] = block[
                    q * GROUP : (q + 1) * GROUP, h * LANES : (h + 1) * LANES
                ]
        return carry

    lax.fori_loop(0, rf.shape[0] // piece, halve, 0)

    def column(ref, start):
        return jnp.concatenate(
            [ref[pl.ds(start + h * GROUP, parts, stride=tall), :] for h in range(halves)], axis=1
        )

    def inner_transform(real, imag):
        high, low = split(jnp.concatenate([real, imag], axis=1))
        return dot(high, inner_v[0]) + dot(low, inner_v[0]) + dot(high, inner_v[1])

    def channel(chunk, c, carry):
        cosine = table_v[double : double + parts, 0:width]
        sine = table_v[double : double + parts, width:double]
        signals = [
            column(rfh, chunk * GROUP * halves + c),
            column(rmd.at[chunk], c),
            column(rmd.at[chunk], GROUP * halves + c),
        ]
        high, low = split(jnp.concatenate(signals, axis=1))
        spread = dot(first[...], jnp.concatenate([high, low, high], axis=0))
        pairs = [
            turned(
                spread[:parts, s * width : (s + 1) * width],
                spread[parts:, s * width : (s + 1) * width],
                cosine, sine,
            )
            for s in range(3)
        ]
        spectra = inner_transform(
            jnp.concatenate([p[0] for p in pairs], axis=0),
            jnp.concatenate([p[1] for p in pairs], axis=0),
        )
        real, imag = spectra[:, :width], spectra[:, width:]
        sr, si = real[2 * parts :], imag[2 * parts :]
        both_r = [real[s * parts : (s + 1) * parts] * sr + imag[s * parts : (s + 1) * parts] * si for s in (0, 1)]
        both_i = [imag[s * parts : (s + 1) * parts] * sr - real[s * parts : (s + 1) * parts] * si for s in (0, 1)]
        back = inner_transform(jnp.concatenate(both_r, axis=0), jnp.concatenate(both_i, axis=0))
        pairs = [
            turned(back[s * parts : (s + 1) * parts, :width], back[s * parts : (s + 1) * parts, width:], cosine, sine)
            for s in (0, 1)
        ]
        folded = jnp.concatenate(
            [jnp.concatenate([p[0] for p in pairs], axis=1), jnp.concatenate([p[1] for p in pairs], axis=1)],
            axis=0,
        )
        high, low = split(folded)
        result = dot(last[...], jnp.concatenate([high, low, high], axis=0))
        gain = skip_s[me * rows + chunk * GROUP + c]
        both = (result[:, :width] + gain * signals[2], result[:, width:])
        for s in range(2):
            for h in range(halves):
                start = (s * halves + h) * GROUP + c
                res_h[pl.ds(start, parts, stride=tall), :] = both[s][
                    :, h * LANES : (h + 1) * LANES
                ]
        return carry

    def widen(chunk, b, carry):
        for q in range(4):
            block = b * 4 + q
            start = pl.multiple_of(block * tall, tall)
            for s in range(2):
                res[chunk, block, s] = jnp.concatenate(
                    [
                        res_h[pl.ds(start + (s * halves + h) * GROUP, GROUP), :]
                        for h in range(halves)
                    ],
                    axis=1,
                )
        return carry

    def finish(chunk, b, carry):
        for q in range(4):
            block = b * 4 + q
            here = pl.ds(pl.multiple_of(block * rows + chunk * GROUP, GROUP), GROUP)
            back = out[chunk, block, 0]
            grad_key[here, :] = back * values_v[here, :]
            grad_value[here, :] = back * keyed_v[here, :]
            grad_filter[here, :] = out[chunk, block, 1] * ((parts * width) ** -0.5)
        return carry

    for chunk in range(CHUNKS):
        arrived(rmd.at[chunk], 2 + chunk)
        lax.fori_loop(0, GROUP, functools.partial(channel, chunk), 0)
        lax.fori_loop(0, parts // 4, functools.partial(widen, chunk), 0)
        send(lambda i: res.at[chunk, i], lambda i: out.at[chunk, i], 4 + chunk)

    done = cnt_all.at[pl.ds(0, parts - 1)]
    pltpu.make_async_copy(done, done, send_sem.at[0]).wait()
    sent(rf, 1)
    for chunk in range(CHUNKS):
        sent(rmd.at[chunk], 2 + chunk)
    for chunk in range(CHUNKS):
        whole = res.at[chunk]
        done = whole.at[pl.ds(0, parts - 1)]
        pltpu.make_async_copy(done, done, send_sem.at[4 + chunk]).wait()
        arrived(out.at[chunk], 4 + chunk)
        lax.fori_loop(0, parts // 4, functools.partial(finish, chunk), 0)


def on_device(
    token_ids, domain_ids, domain_counts, embed_table, query_act, key_act, conv_saved,
    loss_seed, filters, skip_gain,
):
    parts = lax.axis_size("ctx")
    chans, width = query_act.shape
    vocab = embed_table.shape[0]
    table = jnp.asarray(constants(parts, width))
    vmem = pl.BlockSpec(memory_space=pltpu.VMEM)
    hbm = pl.BlockSpec(memory_space=pltpu.HBM)
    rows = CHUNKS * GROUP
    halves = width // LANES
    assert chans == parts * rows
    hold = jax.ShapeDtypeStruct((chans, width), F32)
    results = pl.pallas_call(
        functools.partial(kernel, parts, width),
        out_shape=(hold,) * 4,
        in_specs=[hbm] * 11,
        out_specs=(vmem,) * 4,
        scratch_shapes=[
            pltpu.VMEM(domain_counts.shape, jnp.int32),
            pltpu.VMEM((1, width), jnp.int32),
            pltpu.VMEM((1, width), jnp.int32),
            pltpu.SMEM((chans,), F32),
            pltpu.VMEM(table.shape, F32),
            pltpu.VMEM((1, LANES), F32),
            pltpu.VMEM((parts, 1, LANES), F32),
            pltpu.VMEM((vocab, chans), BF16),
            pltpu.VMEM((chans, width), BF16),
            pltpu.VMEM((chans, width), BF16),
            pltpu.VMEM((chans, width), BF16),
            pltpu.VMEM((chans, width), BF16),
            pltpu.VMEM((2 * parts, 3 * parts), BF16),
            pltpu.VMEM((parts, 6 * parts), BF16),
            pltpu.VMEM((2, 2 * width, 2 * width), BF16),
            pltpu.VMEM((chans, width), F32),
            pltpu.VMEM((chans, width), F32),
            pltpu.VMEM((CHUNKS, parts, 2, GROUP, width), F32),
            pltpu.VMEM((CHUNKS, chans * halves, LANES), F32),
            pltpu.VMEM((chans, width), F32),
            pltpu.VMEM((chans * halves, LANES), F32),
            pltpu.VMEM((CHUNKS, chans * halves, LANES), F32),
            pltpu.VMEM((chans * halves, LANES), F32),
            pltpu.VMEM((CHUNKS, parts, 2, GROUP, width), F32),
            pltpu.SemaphoreType.DMA((10,)),
            pltpu.SemaphoreType.DMA((6,)),
            pltpu.SemaphoreType.DMA((6,)),
        ],
        compiler_params=pltpu.CompilerParams(
            collective_id=0, has_side_effects=True, vmem_limit_bytes=40 * 2**20
        ),
        name="exchange",
    )(*[
        pltpu.with_memory_space_constraint(x, pltpu.HBM)
        for x in (
            domain_counts, token_ids[None, :], domain_ids[None, :], skip_gain, table,
            embed_table, query_act, key_act, conv_saved, loss_seed, filters,
        )
    ])
    return pl.pallas_call(
        write_out,
        out_shape=(hold,) * 4,
        in_specs=[pl.BlockSpec(memory_space=pl.ANY)] * 4,
        out_specs=(hbm,) * 4,
        scratch_shapes=[pltpu.SemaphoreType.DMA((4,))],
        compiler_params=pltpu.CompilerParams(vmem_limit_bytes=4 * 2**20),
        name="write_out",
    )(*[pltpu.with_memory_space_constraint(x, pltpu.VMEM) for x in results])


def write_out(*refs):
    semaphores = refs[-1]
    copies = [
        pltpu.make_async_copy(refs[i], refs[4 + i], semaphores.at[i]) for i in range(4)
    ]
    for copy in copies:
        copy.start()
    for copy in copies:
        copy.wait()


def solution(mesh):
    in_specs = (
        P("ctx"), P("ctx"), P("ctx", None), P(None, "chan"),
        P("chan", "ctx"), P("chan", "ctx"), P("chan", "ctx"), P("chan", "ctx"), P("chan", "ctx"),
        P("chan"),
    )
    out_specs = (P("chan", "ctx"),) * 4
    return jax.shard_map(
        on_device, mesh=mesh, in_specs=in_specs, out_specs=out_specs, check_vma=False
    )
```

```python
import functools

import jax
import jax.numpy as jnp
import ml_dtypes
import numpy as np
from jax import lax
from jax.experimental import pallas as pl
from jax.experimental.pallas import tpu as pltpu
from jax.sharding import PartitionSpec as P

MESH = pl.DeviceIdType.MESH
F32, BF16 = jnp.float32, jnp.bfloat16
count_unit = 64.0
LANES = 128
GROUP = 8
CHUNKS = 2
BATCH = 4


def split_host(x):
    high = x.astype(np.float32).astype(ml_dtypes.bfloat16)
    low = (x - high.astype(np.float64)).astype(np.float32).astype(ml_dtypes.bfloat16)
    return high, low


def constants(parts, width):
    total = parts * width
    j, r = np.arange(parts), np.arange(width)
    theta = 2.0 * np.pi * np.outer(j + 0.25, j) / parts
    first = np.concatenate([np.cos(theta), -np.sin(theta)], 0)
    phase = 2.0 * np.pi * np.outer(j + 0.25, r) / total
    omega = 2.0 * np.pi * (np.outer(r, r) % width) / width
    cosine, sine = np.cos(omega), np.sin(omega)
    inner = np.block([[cosine, -sine], [sine, cosine]])
    last = np.concatenate([np.cos(theta).T, np.sin(theta).T], 1) / total
    fh, fl = split_host(first)
    lh, ll = split_host(last)
    first_cat = np.concatenate([fh, fh, fl], 1)
    last_cat = np.concatenate([lh, lh, ll], 1)
    table = np.zeros((2 * width + 4 * parts, 2 * width), np.float32)
    table[: 2 * width] = inner
    table[2 * width : 2 * width + parts] = np.concatenate([np.cos(phase), np.sin(phase)], 1)
    table[2 * width + parts : 2 * width + 3 * parts, : 3 * parts] = first_cat
    table[2 * width + 3 * parts :, : 6 * parts] = last_cat
    return table


def split(x):
    high = x.astype(BF16)
    return high, (x - high.astype(F32)).astype(BF16)


def dot(a, b):
    return jnp.dot(a, b, preferred_element_type=F32)


def turned(a, b, cosine, sine):
    return a * cosine + b * sine, b * cosine - a * sine


def kernel(
    parts, width, side,
    counts, tokens, domains, skip, table,
    embed, query, key, saved, loss, filters,
    grad_query, grad_key, grad_value, grad_filter,
    counts_v, tokens_v, domains_v, skip_s, table_v,
    cnt_src, cnt_z, cnt_part, cnt_all,
    embed_v, query_v, key_v, saved_v, loss_v, first, last, inner_v, values_v, keyed_v,
    md, zf, zmd, rf, rfh, rmd, res_h, res, zres, out,
    load_sem, send_sem, recv_sem,
):
    me = lax.axis_index("ctx")
    chan = lax.axis_index("chan")
    x, z, y = me // (side * side), lax.rem(me // side, side), lax.rem(me, side)
    plane = side * side
    rows = CHUNKS * GROUP
    halves = width // LANES
    tall = rows * halves
    steps = (2, 1, 3)
    barrier = pltpu.get_barrier_semaphore()

    def along(k):
        return lax.rem(z + k, side)

    def z_peer(k):
        return (x * plane + along(k) * side + y, chan)

    def beside(i):
        return lax.rem(x + i // side, side), lax.rem(y + i, side)

    def xy_peer(i):
        xx, yy = beside(i)
        return (xx * plane + z * side + yy, chan)

    def greet(i, carry):
        pl.semaphore_signal(barrier, inc=1, device_id=xy_peer(i), device_id_type=MESH)
        return carry

    for k in steps:
        pl.semaphore_signal(barrier, inc=1, device_id=z_peer(k), device_id_type=MESH)
    lax.fori_loop(1, plane, greet, 0)

    loads = [
        pltpu.make_async_copy(source, target, load_sem.at[i])
        for i, (source, target) in enumerate(
            [
                (counts, counts_v), (tokens, tokens_v), (domains, domains_v), (embed, embed_v),
                (key, key_v), (query, query_v), (saved, saved_v), (loss, loss_v),
                (skip, skip_s), (table, table_v),
            ]
        )
    ]
    for load in loads:
        load.start()
    domain_count = counts.shape[1]
    cnt_src[...] = jnp.zeros_like(cnt_src)
    loads[0].wait()
    cnt_src[0:1, 0:domain_count] = counts_v[...].astype(F32)

    def remote(source, target, slot, peer):
        pltpu.make_async_remote_copy(
            src_ref=source, dst_ref=target, send_sem=send_sem.at[slot], recv_sem=recv_sem.at[slot],
            device_id=peer, device_id_type=MESH,
        ).start()

    def spread_plane(source, target, slot):
        pltpu.make_async_copy(source(x, y), target, recv_sem.at[slot]).start()

        def go(i, carry):
            remote(source(*beside(i)), target, slot, xy_peer(i))
            return carry

        lax.fori_loop(1, plane, go, 0)

    def taken(like, slot, sem):
        pltpu.make_async_copy(like, like, sem.at[slot]).wait()

    def piece_of(ref, index, size):
        return ref.at[pl.ds(pl.multiple_of(index * size, size), size)]

    def source_index(k):
        return x * plane + lax.rem(z + side - k, side) * side + y

    cnt_slot, f_slot, md_slot, res_slot, end_slot = 0, (2, 22), (6, 10), (14, 17), (20, 21)

    pl.semaphore_wait(barrier, plane - 1 + side - 1)

    for k in steps:
        remote(cnt_src, cnt_z.at[k - 1], cnt_slot, z_peer(k))

    def send_filters(chunk):
        for k in steps:
            remote(
                filters.at[:, along(k), :, chunk], zf.at[chunk, k - 1], f_slot[chunk] + k, z_peer(k)
            )
        spread_plane(
            lambda xx, yy: filters.at[xx, z, yy, chunk],
            piece_of(rf.at[chunk], source_index(0), GROUP),
            f_slot[chunk],
        )

    def forward_filters(chunk, k):
        taken(zf.at[chunk, k - 1], f_slot[chunk] + k, recv_sem)
        spread_plane(
            lambda xx, yy: zf.at[chunk, k - 1, xx, yy],
            piece_of(rf.at[chunk], source_index(k), GROUP),
            f_slot[chunk],
        )

    send_filters(0)

    for load in loads[1:4]:
        load.wait()
    vocab = embed_v.shape[0]
    onehot = (
        lax.broadcasted_iota(jnp.int32, (vocab, width), 0) == tokens_v[...]
    ).astype(F32).astype(BF16)
    piece = 128

    def look_up(b, carry):
        at = pl.multiple_of(b * piece, piece)
        values_v[pl.ds(at, piece), :] = lax.dot_general(
            embed_v[:, pl.ds(at, piece)], onehot, (((0,), (0,)), ((), ())),
            preferred_element_type=F32,
        )
        return carry

    taken(cnt_z, cnt_slot, recv_sem)
    cnt_part[...] = cnt_src[...] + cnt_z[0] + cnt_z[1] + cnt_z[2]
    spread_plane(lambda xx, yy: cnt_part, cnt_all.at[x * side + y], cnt_slot + 1)
    lax.fori_loop(0, values_v.shape[0] // piece, look_up, 0)
    for load in loads[4:8]:
        load.wait()
    taken(cnt_all, cnt_slot + 1, recv_sem)
    totals = jnp.sum(cnt_all[...], axis=0)
    shares = (count_unit * parts) / totals
    weight = jnp.zeros((1, width), F32)
    for d in range(domain_count):
        weight = jnp.where(domains_v[...] == d, shares[0:1, d : d + 1], weight)

    def products(b, carry):
        at = pl.multiple_of(b * piece, piece)
        block = pl.ds(at, piece)
        keyed = key_v[block, :].astype(F32)
        keyed_v[block, :] = keyed
        mixed = keyed * values_v[block, :]
        upstream = (loss_v[block, :].astype(F32) * weight).astype(BF16).astype(F32)
        grad_query[block, :] = upstream * saved_v[block, :].astype(F32)
        dconv = upstream * query_v[block, :].astype(F32)
        for q in range(piece // rows):
            owner = b * (piece // rows) + q
            ox, oz, oy = owner // plane, lax.rem(owner // side, side), q % side
            for chunk in range(CHUNKS):
                part = slice(q * rows + chunk * GROUP, q * rows + (chunk + 1) * GROUP)
                for h in range(halves):
                    start = oy * tall + h * GROUP
                    lanes = slice(h * LANES, (h + 1) * LANES)
                    md[chunk, ox, oz, start : start + GROUP, :] = mixed[part, lanes]
                    start = start + halves * GROUP
                    md[chunk, ox, oz, start : start + GROUP, :] = dconv[part, lanes]
        return carry

    lax.fori_loop(0, values_v.shape[0] // piece, products, 0)

    def send_signals(chunk):
        for k in steps:
            remote(md.at[chunk, :, along(k)], zmd.at[chunk, k - 1], md_slot[chunk] + k, z_peer(k))
        spread_plane(
            lambda xx, yy: piece_of(md.at[chunk, xx, z], yy, tall),
            piece_of(rmd.at[chunk], source_index(0), tall),
            md_slot[chunk],
        )

    def forward_signals(chunk, k):
        taken(zmd.at[chunk, k - 1], md_slot[chunk] + k, recv_sem)
        spread_plane(
            lambda xx, yy: piece_of(zmd.at[chunk, k - 1, xx], yy, tall),
            piece_of(rmd.at[chunk], source_index(k), tall),
            md_slot[chunk],
        )

    send_signals(0)
    for k in steps:
        forward_filters(0, k)

    for load in loads[8:]:
        load.wait()
    double = 2 * width
    first[...] = table_v[double + parts : double + 3 * parts, 0 : 3 * parts].astype(BF16)
    last[...] = table_v[double + 3 * parts : double + 4 * parts, 0 : 6 * parts].astype(BF16)
    inner_v[0], inner_v[1] = split(table_v[0:double, :])
    for k in steps:
        forward_signals(0, k)
        if k == steps[1]:
            send_filters(1)
    send_signals(1)

    def halve(chunk, b, carry):
        at = pl.multiple_of(b * piece, piece)
        block = rf[chunk, pl.ds(at, piece), :]
        for q in range(piece // GROUP):
            for h in range(halves):
                start = pl.multiple_of((at + q * GROUP) * halves + h * GROUP, GROUP)
                rfh[chunk, pl.ds(start, GROUP), :] = block[
                    q * GROUP : (q + 1) * GROUP, h * LANES : (h + 1) * LANES
                ]
        return carry

    def column(ref, start, stride):
        return jnp.concatenate(
            [ref[pl.ds(start + h * GROUP, parts, stride=stride), :] for h in range(halves)], axis=1
        )

    def inner_transform(real, imag):
        high, low = split(jnp.concatenate([real, imag], axis=1))
        count = high.shape[0]
        coarse = dot(jnp.concatenate([high, low], axis=0), inner_v[0])
        return coarse[:count] + coarse[count:] + dot(high, inner_v[1])

    def channels(chunk, g, carry):
        cosine = table_v[double : double + parts, 0:width]
        sine = table_v[double : double + parts, width:double]
        lines = [[], [], []]
        for p in range(BATCH):
            c = g * BATCH + p
            lines[0].append(column(rfh.at[chunk], c, GROUP * halves))
            lines[1].append(column(rmd.at[chunk], c, tall))
            lines[2].append(column(rmd.at[chunk], GROUP * halves + c, tall))
        turns = [[], [], []]
        for p in range(BATCH):
            high, low = split(jnp.concatenate([line[p] for line in lines], axis=1))
            spread = dot(first[...], jnp.concatenate([high, low, high], axis=0))
            for s in range(3):
                turns[s].append(
                    turned(
                        spread[:parts, s * width : (s + 1) * width],
                        spread[parts:, s * width : (s + 1) * width],
                        cosine, sine,
                    )
                )
        flat = turns[0] + turns[1] + turns[2]
        spectra = inner_transform(
            jnp.concatenate([t[0] for t in flat], axis=0),
            jnp.concatenate([t[1] for t in flat], axis=0),
        )
        real, imag = spectra[:, :width], spectra[:, width:]
        batch = BATCH * parts
        sr, si = real[2 * batch :], imag[2 * batch :]
        both_r = [real[s * batch : (s + 1) * batch] * sr + imag[s * batch : (s + 1) * batch] * si for s in (0, 1)]
        both_i = [imag[s * batch : (s + 1) * batch] * sr - real[s * batch : (s + 1) * batch] * si for s in (0, 1)]
        back = inner_transform(jnp.concatenate(both_r, axis=0), jnp.concatenate(both_i, axis=0))
        for p in range(BATCH):
            pairs = []
            for s in (0, 1):
                at = s * batch + p * parts
                pairs.append(turned(back[at : at + parts, :width], back[at : at + parts, width:], cosine, sine))
            folded = jnp.concatenate(
                [jnp.concatenate([t[0] for t in pairs], axis=1), jnp.concatenate([t[1] for t in pairs], axis=1)],
                axis=0,
            )
            high, low = split(folded)
            result = dot(last[...], jnp.concatenate([high, low, high], axis=0))
            c = g * BATCH + p
            gain = skip_s[me * rows + chunk * GROUP + c]
            both = (result[:, :width] + gain * lines[2][p], result[:, width:])
            for s in range(2):
                for h in range(halves):
                    start = (s * halves + h) * GROUP + c
                    res_h[pl.ds(start, parts, stride=tall), :] = both[s][
                        :, h * LANES : (h + 1) * LANES
                    ]
        return carry

    def widen(chunk, zz, xx, carry):
        for yy in range(side):
            start = pl.multiple_of((xx * plane + zz * side + yy) * tall, tall)
            for s in range(2):
                res[chunk, xx, zz, yy, s] = jnp.concatenate(
                    [
                        res_h[pl.ds(start + (s * halves + h) * GROUP, GROUP), :]
                        for h in range(halves)
                    ],
                    axis=1,
                )
        return carry

    def finish(chunk, b, carry):
        for q in range(side):
            here = pl.ds(pl.multiple_of((b * side + q) * rows + chunk * GROUP, GROUP), GROUP)
            ox, oz = b // side, lax.rem(b, side)
            back = out[chunk, ox, oz, q, 0]
            grad_key[here, :] = back * values_v[here, :]
            grad_value[here, :] = back * keyed_v[here, :]
            grad_filter[here, :] = out[chunk, ox, oz, q, 1] * ((parts * width) ** -0.5)
        return carry

    def transform(chunk):
        taken(rf.at[chunk], f_slot[chunk], recv_sem)
        lax.fori_loop(0, rf.shape[1] // piece, functools.partial(halve, chunk), 0)
        taken(rmd.at[chunk], md_slot[chunk], recv_sem)
        lax.fori_loop(0, GROUP // BATCH, functools.partial(channels, chunk), 0)
        for k in steps + (0,):
            zz = along(k)
            lax.fori_loop(0, side, functools.partial(widen, chunk, zz), 0)
            spread_plane(
                lambda xx, yy: res.at[chunk, xx, zz, yy],
                zres.at[chunk, k - 1, x, y] if k else out.at[chunk, x, z, y],
                res_slot[chunk] + k - 1 if k else end_slot[chunk],
            )

    def forward_results(chunk, k):
        taken(zres.at[chunk, k - 1], res_slot[chunk] + k - 1, recv_sem)
        remote(zres.at[chunk, k - 1], out.at[chunk, :, z], end_slot[chunk], z_peer(k))

    transform(0)
    for k in steps:
        forward_filters(1, k)
    for k in steps:
        forward_signals(1, k)
        forward_results(0, k)
    transform(1)
    for k in steps:
        forward_results(1, k)

    taken(cnt_z, cnt_slot, send_sem)
    taken(cnt_all.at[pl.ds(0, plane - 1)], cnt_slot + 1, send_sem)
    for chunk in range(CHUNKS):
        for k in steps:
            taken(zf.at[chunk, k - 1], f_slot[chunk] + k, send_sem)
            taken(zmd.at[chunk, k - 1], md_slot[chunk] + k, send_sem)
            taken(rmd.at[chunk, pl.ds(0, (plane - 1) * tall)], res_slot[chunk] + k - 1, send_sem)
        taken(rf.at[chunk, pl.ds(0, (parts - side) * GROUP)], f_slot[chunk], send_sem)
        taken(rmd.at[chunk, pl.ds(0, (parts - side) * tall)], md_slot[chunk], send_sem)
    for chunk in range(CHUNKS):
        taken(out.at[chunk], end_slot[chunk], recv_sem)
        lax.fori_loop(0, plane, functools.partial(finish, chunk), 0)
    for chunk in range(CHUNKS):
        taken(rmd.at[chunk, pl.ds(0, (parts - 1) * tall)], end_slot[chunk], send_sem)


def on_device(
    token_ids, domain_ids, domain_counts, embed_table, query_act, key_act, conv_saved,
    loss_seed, filters, skip_gain,
):
    parts = lax.axis_size("ctx")
    chans, width = query_act.shape
    vocab = embed_table.shape[0]
    table = jnp.asarray(constants(parts, width))
    vmem = pl.BlockSpec(memory_space=pltpu.VMEM)
    hbm = pl.BlockSpec(memory_space=pltpu.HBM)
    rows = CHUNKS * GROUP
    halves = width // LANES
    side = 4
    assert chans == parts * rows and parts == side**3
    block = (2, GROUP, width)
    hold = jax.ShapeDtypeStruct((chans, width), F32)
    results = pl.pallas_call(
        functools.partial(kernel, parts, width, side),
        out_shape=(hold,) * 4,
        in_specs=[hbm] * 11,
        out_specs=(vmem,) * 4,
        scratch_shapes=[
            pltpu.VMEM(domain_counts.shape, jnp.int32),
            pltpu.VMEM((1, width), jnp.int32),
            pltpu.VMEM((1, width), jnp.int32),
            pltpu.SMEM((chans,), F32),
            pltpu.VMEM(table.shape, F32),
            pltpu.VMEM((1, LANES), F32),
            pltpu.VMEM((side - 1, 1, LANES), F32),
            pltpu.VMEM((1, LANES), F32),
            pltpu.VMEM((side**2, 1, LANES), F32),
            pltpu.VMEM((vocab, chans), BF16),
            pltpu.VMEM((chans, width), BF16),
            pltpu.VMEM((chans, width), BF16),
            pltpu.VMEM((chans, width), BF16),
            pltpu.VMEM((chans, width), BF16),
            pltpu.VMEM((2 * parts, 3 * parts), BF16),
            pltpu.VMEM((parts, 6 * parts), BF16),
            pltpu.VMEM((2, 2 * width, 2 * width), BF16),
            pltpu.VMEM((chans, width), F32),
            pltpu.VMEM((chans, width), F32),
            pltpu.VMEM((CHUNKS, side, side, side * rows * halves, LANES), F32),
            pltpu.VMEM((CHUNKS, side - 1, side, side, GROUP, width), F32),
            pltpu.VMEM((CHUNKS, side - 1, side, side * rows * halves, LANES), F32),
            pltpu.VMEM((CHUNKS, parts * GROUP, width), F32),
            pltpu.VMEM((CHUNKS, parts * GROUP * halves, LANES), F32),
            pltpu.VMEM((CHUNKS, chans * halves, LANES), F32),
            pltpu.VMEM((chans * halves, LANES), F32),
            pltpu.VMEM((CHUNKS, side, side, side) + block, F32),
            pltpu.VMEM((CHUNKS, side - 1, side, side) + block, F32),
            pltpu.VMEM((CHUNKS, side, side, side) + block, F32),
            pltpu.SemaphoreType.DMA((10,)),
            pltpu.SemaphoreType.DMA((26,)),
            pltpu.SemaphoreType.DMA((26,)),
        ],
        compiler_params=pltpu.CompilerParams(
            collective_id=0, has_side_effects=True, vmem_limit_bytes=44 * 2**20
        ),
        name="exchange",
    )(*[
        pltpu.with_memory_space_constraint(x, pltpu.HBM)
        for x in (
            domain_counts, token_ids[None, :], domain_ids[None, :], skip_gain, table,
            embed_table, query_act, key_act, conv_saved, loss_seed,
            filters.reshape(side, side, side, CHUNKS, GROUP, width),
        )
    ])
    return pl.pallas_call(
        write_out,
        out_shape=(hold,) * 4,
        in_specs=[pl.BlockSpec(memory_space=pl.ANY)] * 4,
        out_specs=(hbm,) * 4,
        scratch_shapes=[pltpu.SemaphoreType.DMA((4,))],
        compiler_params=pltpu.CompilerParams(vmem_limit_bytes=4 * 2**20),
        name="write_out",
    )(*[pltpu.with_memory_space_constraint(x, pltpu.VMEM) for x in results])


def write_out(*refs):
    semaphores = refs[-1]
    copies = [
        pltpu.make_async_copy(refs[i], refs[4 + i], semaphores.at[i]) for i in range(4)
    ]
    for copy in copies:
        copy.start()
    for copy in copies:
        copy.wait()


def solution(mesh):
    in_specs = (
        P("ctx"), P("ctx"), P("ctx", None), P(None, "chan"),
        P("chan", "ctx"), P("chan", "ctx"), P("chan", "ctx"), P("chan", "ctx"), P("chan", "ctx"),
        P("chan"),
    )
    out_specs = (P("chan", "ctx"),) * 4
    return jax.shard_map(
        on_device, mesh=mesh, in_specs=in_specs, out_specs=out_specs, check_vma=False
    )
```

```python
import functools

import jax
import jax.numpy as jnp
import ml_dtypes
import numpy as np
from jax import lax
from jax.experimental import pallas as pl
from jax.experimental.pallas import tpu as pltpu
from jax.sharding import PartitionSpec as P

MESH = pl.DeviceIdType.MESH
F32, BF16 = jnp.float32, jnp.bfloat16
count_unit = 64.0
LANES = 128
GROUP = 8
CHUNKS = 2
BATCH = 4


def split_host(x):
    high = x.astype(np.float32).astype(ml_dtypes.bfloat16)
    low = (x - high.astype(np.float64)).astype(np.float32).astype(ml_dtypes.bfloat16)
    return high, low


def constants(parts, width):
    total = parts * width
    j, r = np.arange(parts), np.arange(width)
    theta = 2.0 * np.pi * np.outer(j + 0.25, j) / parts
    first = np.concatenate([np.cos(theta), -np.sin(theta)], 0)
    phase = 2.0 * np.pi * np.outer(j + 0.25, r) / total
    omega = 2.0 * np.pi * (np.outer(r, r) % width) / width
    cosine, sine = np.cos(omega), np.sin(omega)
    inner = np.block([[cosine, -sine], [sine, cosine]])
    last = np.concatenate([np.cos(theta).T, np.sin(theta).T], 1) / total
    fh, fl = split_host(first)
    lh, ll = split_host(last)
    first_cat = np.concatenate([fh, fh, fl], 1)
    last_cat = np.concatenate([lh, lh, ll], 1)
    table = np.zeros((2 * width + 4 * parts, 2 * width), np.float32)
    table[: 2 * width] = inner
    table[2 * width : 2 * width + parts] = np.concatenate([np.cos(phase), np.sin(phase)], 1)
    table[2 * width + parts : 2 * width + 3 * parts, : 3 * parts] = first_cat
    table[2 * width + 3 * parts :, : 6 * parts] = last_cat
    return table


def split(x):
    high = x.astype(BF16)
    return high, (x - high.astype(F32)).astype(BF16)


def dot(a, b):
    return jnp.dot(a, b, preferred_element_type=F32)


def turned(a, b, cosine, sine):
    return a * cosine + b * sine, b * cosine - a * sine


def kernel(
    parts, width, side,
    counts, tokens, domains, skip, table,
    embed, query, key, saved, loss, filters,
    grad_query, grad_key, grad_value, grad_filter,
    counts_v, tokens_v, domains_v, skip_s, table_v,
    cnt_src, cnt_z, cnt_part, cnt_all,
    embed_v, query_v, key_v, saved_v, loss_v, first, last, inner_v, values_v, keyed_v,
    md, zf, zmd, rf, rfh, rmd, res_h, res, zres, out,
    load_sem, send_sem, recv_sem,
):
    me = lax.axis_index("ctx")
    chan = lax.axis_index("chan")
    x, z, y = me // (side * side), lax.rem(me // side, side), lax.rem(me, side)
    plane = side * side
    rows = CHUNKS * GROUP
    halves = width // LANES
    tall = rows * halves
    steps = (1, 2, 3)
    barrier = pltpu.get_barrier_semaphore()

    def along(k):
        return lax.rem(z + k, side)

    def z_peer(k):
        return (x * plane + along(k) * side + y, chan)

    def beside(i):
        return lax.rem(x + i // side, side), lax.rem(y + i, side)

    def xy_peer(i):
        xx, yy = beside(i)
        return (xx * plane + z * side + yy, chan)

    def greet(i, carry):
        pl.semaphore_signal(barrier, inc=1, device_id=xy_peer(i), device_id_type=MESH)
        return carry

    for k in steps:
        pl.semaphore_signal(barrier, inc=1, device_id=z_peer(k), device_id_type=MESH)
    lax.fori_loop(1, plane, greet, 0)

    loads = [
        pltpu.make_async_copy(source, target, load_sem.at[i])
        for i, (source, target) in enumerate(
            [
                (counts, counts_v), (tokens, tokens_v), (domains, domains_v), (embed, embed_v),
                (key, key_v), (query, query_v), (saved, saved_v), (loss, loss_v),
                (skip, skip_s), (table, table_v),
            ]
        )
    ]
    for load in loads:
        load.start()
    domain_count = counts.shape[1]
    cnt_src[...] = jnp.zeros_like(cnt_src)
    loads[0].wait()
    cnt_src[0:1, 0:domain_count] = counts_v[...].astype(F32)

    def remote(source, target, slot, peer):
        pltpu.make_async_remote_copy(
            src_ref=source, dst_ref=target, send_sem=send_sem.at[slot], recv_sem=recv_sem.at[slot],
            device_id=peer, device_id_type=MESH,
        ).start()

    def spread_plane(source, target, slot):
        pltpu.make_async_copy(source(x, y), target, recv_sem.at[slot]).start()

        def go(i, carry):
            remote(source(*beside(i)), target, slot, xy_peer(i))
            return carry

        lax.fori_loop(1, plane, go, 0)

    def taken(like, slot, sem):
        pltpu.make_async_copy(like, like, sem.at[slot]).wait()

    def piece_of(ref, index, size):
        return ref.at[pl.ds(pl.multiple_of(index * size, size), size)]

    def source_index(k):
        return x * plane + lax.rem(z + side - k, side) * side + y

    cnt_slot, f_slot, md_slot, res_slot, end_slot = 0, (2, 22), (6, 10), (14, 17), (26, 27)

    pl.semaphore_wait(barrier, plane - 1 + side - 1)

    for k in steps:
        remote(cnt_src, cnt_z.at[k - 1], cnt_slot, z_peer(k))

    def send_filters(chunk):
        for k in steps:
            remote(
                filters.at[:, along(k), :, chunk], zf.at[chunk, k - 1], f_slot[chunk] + k, z_peer(k)
            )
        spread_plane(
            lambda xx, yy: filters.at[xx, z, yy, chunk],
            piece_of(rf.at[chunk], source_index(0), GROUP),
            f_slot[chunk],
        )

    def forward_filters(chunk, k):
        taken(zf.at[chunk, k - 1], f_slot[chunk] + k, recv_sem)
        spread_plane(
            lambda xx, yy: zf.at[chunk, k - 1, xx, yy],
            piece_of(rf.at[chunk], source_index(k), GROUP),
            f_slot[chunk],
        )

    send_filters(0)

    for load in loads[1:4]:
        load.wait()
    vocab = embed_v.shape[0]
    onehot = (
        lax.broadcasted_iota(jnp.int32, (vocab, width), 0) == tokens_v[...]
    ).astype(F32).astype(BF16)
    piece = 128

    def look_up(b, carry):
        at = pl.multiple_of(b * piece, piece)
        values_v[pl.ds(at, piece), :] = lax.dot_general(
            embed_v[:, pl.ds(at, piece)], onehot, (((0,), (0,)), ((), ())),
            preferred_element_type=F32,
        )
        return carry

    taken(cnt_z, cnt_slot, recv_sem)
    cnt_part[...] = cnt_src[...] + cnt_z[0] + cnt_z[1] + cnt_z[2]
    spread_plane(lambda xx, yy: cnt_part, cnt_all.at[x * side + y], cnt_slot + 1)
    lax.fori_loop(0, values_v.shape[0] // piece, look_up, 0)
    for load in loads[4:8]:
        load.wait()
    taken(cnt_all, cnt_slot + 1, recv_sem)
    totals = jnp.sum(cnt_all[...], axis=0)
    shares = (count_unit * parts) / totals
    weight = jnp.zeros((1, width), F32)
    for d in range(domain_count):
        weight = jnp.where(domains_v[...] == d, shares[0:1, d : d + 1], weight)

    def products(b, carry):
        at = pl.multiple_of(b * piece, piece)
        block = pl.ds(at, piece)
        keyed = key_v[block, :].astype(F32)
        keyed_v[block, :] = keyed
        mixed = keyed * values_v[block, :]
        upstream = (loss_v[block, :].astype(F32) * weight).astype(BF16).astype(F32)
        grad_query[block, :] = upstream * saved_v[block, :].astype(F32)
        dconv = upstream * query_v[block, :].astype(F32)
        for q in range(piece // rows):
            owner = b * (piece // rows) + q
            ox, oz, oy = owner // plane, lax.rem(owner // side, side), q % side
            for chunk in range(CHUNKS):
                part = slice(q * rows + chunk * GROUP, q * rows + (chunk + 1) * GROUP)
                for h in range(halves):
                    start = oy * tall + h * GROUP
                    lanes = slice(h * LANES, (h + 1) * LANES)
                    md[chunk, ox, oz, start : start + GROUP, :] = mixed[part, lanes]
                    start = start + halves * GROUP
                    md[chunk, ox, oz, start : start + GROUP, :] = dconv[part, lanes]
        return carry

    lax.fori_loop(0, values_v.shape[0] // piece, products, 0)

    def send_signals(chunk):
        for k in steps:
            remote(md.at[chunk, :, along(k)], zmd.at[chunk, k - 1], md_slot[chunk] + k, z_peer(k))
        spread_plane(
            lambda xx, yy: piece_of(md.at[chunk, xx, z], yy, tall),
            piece_of(rmd.at[chunk], source_index(0), tall),
            md_slot[chunk],
        )

    def forward_signals(chunk, k):
        taken(zmd.at[chunk, k - 1], md_slot[chunk] + k, recv_sem)
        spread_plane(
            lambda xx, yy: piece_of(zmd.at[chunk, k - 1, xx], yy, tall),
            piece_of(rmd.at[chunk], source_index(k), tall),
            md_slot[chunk],
        )

    send_signals(0)
    for k in steps:
        forward_filters(0, k)

    for load in loads[8:]:
        load.wait()
    double = 2 * width
    first[...] = table_v[double + parts : double + 3 * parts, 0 : 3 * parts].astype(BF16)
    last[...] = table_v[double + 3 * parts : double + 4 * parts, 0 : 6 * parts].astype(BF16)
    inner_v[0], inner_v[1] = split(table_v[0:double, :])
    for k in steps:
        forward_signals(0, k)
        if k == steps[1]:
            send_filters(1)
    send_signals(1)

    def halve(chunk, b, carry):
        at = pl.multiple_of(b * piece, piece)
        block = rf[chunk, pl.ds(at, piece), :]
        for q in range(piece // GROUP):
            for h in range(halves):
                start = pl.multiple_of((at + q * GROUP) * halves + h * GROUP, GROUP)
                rfh[chunk, pl.ds(start, GROUP), :] = block[
                    q * GROUP : (q + 1) * GROUP, h * LANES : (h + 1) * LANES
                ]
        return carry

    def column(ref, start, stride):
        return jnp.concatenate(
            [ref[pl.ds(start + h * GROUP, parts, stride=stride), :] for h in range(halves)], axis=1
        )

    def inner_transform(real, imag):
        high, low = split(jnp.concatenate([real, imag], axis=1))
        count = high.shape[0]
        coarse = dot(jnp.concatenate([high, low], axis=0), inner_v[0])
        return coarse[:count] + coarse[count:] + dot(high, inner_v[1])

    def channels(chunk, g, carry):
        cosine = table_v[double : double + parts, 0:width]
        sine = table_v[double : double + parts, width:double]
        lines = [[], [], []]
        for p in range(BATCH):
            c = g * BATCH + p
            lines[0].append(column(rfh.at[chunk], c, GROUP * halves))
            lines[1].append(column(rmd.at[chunk], c, tall))
            lines[2].append(column(rmd.at[chunk], GROUP * halves + c, tall))
        turns = [[], [], []]
        for p in range(BATCH):
            high, low = split(jnp.concatenate([line[p] for line in lines], axis=1))
            spread = dot(first[...], jnp.concatenate([high, low, high], axis=0))
            for s in range(3):
                turns[s].append(
                    turned(
                        spread[:parts, s * width : (s + 1) * width],
                        spread[parts:, s * width : (s + 1) * width],
                        cosine, sine,
                    )
                )
        flat = turns[0] + turns[1] + turns[2]
        spectra = inner_transform(
            jnp.concatenate([t[0] for t in flat], axis=0),
            jnp.concatenate([t[1] for t in flat], axis=0),
        )
        real, imag = spectra[:, :width], spectra[:, width:]
        batch = BATCH * parts
        sr, si = real[2 * batch :], imag[2 * batch :]
        both_r = [real[s * batch : (s + 1) * batch] * sr + imag[s * batch : (s + 1) * batch] * si for s in (0, 1)]
        both_i = [imag[s * batch : (s + 1) * batch] * sr - real[s * batch : (s + 1) * batch] * si for s in (0, 1)]
        back = inner_transform(jnp.concatenate(both_r, axis=0), jnp.concatenate(both_i, axis=0))
        for p in range(BATCH):
            pairs = []
            for s in (0, 1):
                at = s * batch + p * parts
                pairs.append(turned(back[at : at + parts, :width], back[at : at + parts, width:], cosine, sine))
            folded = jnp.concatenate(
                [jnp.concatenate([t[0] for t in pairs], axis=1), jnp.concatenate([t[1] for t in pairs], axis=1)],
                axis=0,
            )
            high, low = split(folded)
            result = dot(last[...], jnp.concatenate([high, low, high], axis=0))
            c = g * BATCH + p
            gain = skip_s[me * rows + chunk * GROUP + c]
            both = (result[:, :width] + gain * lines[2][p], result[:, width:])
            for s in range(2):
                for h in range(halves):
                    start = (s * halves + h) * GROUP + c
                    res_h[pl.ds(start, parts, stride=tall), :] = both[s][
                        :, h * LANES : (h + 1) * LANES
                    ]
        return carry

    def widen(chunk, zz, xx, carry):
        for yy in range(side):
            start = pl.multiple_of((xx * plane + zz * side + yy) * tall, tall)
            for s in range(2):
                res[chunk, xx, zz, yy, s] = jnp.concatenate(
                    [
                        res_h[pl.ds(start + (s * halves + h) * GROUP, GROUP), :]
                        for h in range(halves)
                    ],
                    axis=1,
                )
        return carry

    def finish(chunk, oz, ox, carry):
        for q in range(side):
            here = pl.ds(
                pl.multiple_of(((ox * side + oz) * side + q) * rows + chunk * GROUP, GROUP), GROUP
            )
            back = out[chunk, ox, oz, q, 0]
            grad_key[here, :] = back * values_v[here, :]
            grad_value[here, :] = back * keyed_v[here, :]
            grad_filter[here, :] = out[chunk, ox, oz, q, 1] * ((parts * width) ** -0.5)
        return carry

    def transform(chunk):
        taken(rf.at[chunk], f_slot[chunk], recv_sem)
        lax.fori_loop(0, rf.shape[1] // piece, functools.partial(halve, chunk), 0)
        taken(rmd.at[chunk], md_slot[chunk], recv_sem)
        lax.fori_loop(0, GROUP // BATCH, functools.partial(channels, chunk), 0)
        for k in steps + (0,):
            zz = along(k)
            lax.fori_loop(0, side, functools.partial(widen, chunk, zz), 0)
            spread_plane(
                lambda xx, yy: res.at[chunk, xx, zz, yy],
                zres.at[chunk, k - 1, x, y] if k else out.at[chunk, x, z, y],
                res_slot[chunk] + k - 1 if k else end_slot[chunk],
            )

    def forward_results(chunk, k):
        taken(zres.at[chunk, k - 1], res_slot[chunk] + k - 1, recv_sem)
        remote(zres.at[chunk, k - 1], out.at[chunk, :, z], end_slot[chunk] + 2 * k, z_peer(k))

    transform(0)
    for k in steps:
        forward_filters(1, k)
    for k in steps:
        forward_signals(1, k)
        forward_results(0, k)
    transform(1)
    for k in steps:
        forward_results(1, k)

    taken(cnt_z, cnt_slot, send_sem)
    taken(cnt_all.at[pl.ds(0, plane - 1)], cnt_slot + 1, send_sem)
    for chunk in range(CHUNKS):
        for k in steps:
            taken(zf.at[chunk, k - 1], f_slot[chunk] + k, send_sem)
            taken(zmd.at[chunk, k - 1], md_slot[chunk] + k, send_sem)
            taken(rmd.at[chunk, pl.ds(0, (plane - 1) * tall)], res_slot[chunk] + k - 1, send_sem)
        taken(rf.at[chunk, pl.ds(0, (parts - side) * GROUP)], f_slot[chunk], send_sem)
        taken(rmd.at[chunk, pl.ds(0, (parts - side) * tall)], md_slot[chunk], send_sem)
    for chunk in range(CHUNKS):
        for k in (0,) + steps:
            oz = lax.rem(z + side - k, side)
            taken(out.at[chunk, :, oz], end_slot[chunk] + 2 * k, recv_sem)
            lax.fori_loop(0, side, functools.partial(finish, chunk, oz), 0)
    for chunk in range(CHUNKS):
        taken(rmd.at[chunk, pl.ds(0, (plane - 1) * tall)], end_slot[chunk], send_sem)
        for k in steps:
            taken(zres.at[chunk, k - 1], end_slot[chunk] + 2 * k, send_sem)


def on_device(
    token_ids, domain_ids, domain_counts, embed_table, query_act, key_act, conv_saved,
    loss_seed, filters, skip_gain,
):
    parts = lax.axis_size("ctx")
    chans, width = query_act.shape
    vocab = embed_table.shape[0]
    table = jnp.asarray(constants(parts, width))
    vmem = pl.BlockSpec(memory_space=pltpu.VMEM)
    hbm = pl.BlockSpec(memory_space=pltpu.HBM)
    rows = CHUNKS * GROUP
    halves = width // LANES
    side = 4
    assert chans == parts * rows and parts == side**3
    block = (2, GROUP, width)
    hold = jax.ShapeDtypeStruct((chans, width), F32)
    results = pl.pallas_call(
        functools.partial(kernel, parts, width, side),
        out_shape=(hold,) * 4,
        in_specs=[hbm] * 11,
        out_specs=(vmem,) * 4,
        scratch_shapes=[
            pltpu.VMEM(domain_counts.shape, jnp.int32),
            pltpu.VMEM((1, width), jnp.int32),
            pltpu.VMEM((1, width), jnp.int32),
            pltpu.SMEM((chans,), F32),
            pltpu.VMEM(table.shape, F32),
            pltpu.VMEM((1, LANES), F32),
            pltpu.VMEM((side - 1, 1, LANES), F32),
            pltpu.VMEM((1, LANES), F32),
            pltpu.VMEM((side**2, 1, LANES), F32),
            pltpu.VMEM((vocab, chans), BF16),
            pltpu.VMEM((chans, width), BF16),
            pltpu.VMEM((chans, width), BF16),
            pltpu.VMEM((chans, width), BF16),
            pltpu.VMEM((chans, width), BF16),
            pltpu.VMEM((2 * parts, 3 * parts), BF16),
            pltpu.VMEM((parts, 6 * parts), BF16),
            pltpu.VMEM((2, 2 * width, 2 * width), BF16),
            pltpu.VMEM((chans, width), F32),
            pltpu.VMEM((chans, width), F32),
            pltpu.VMEM((CHUNKS, side, side, side * rows * halves, LANES), F32),
            pltpu.VMEM((CHUNKS, side - 1, side, side, GROUP, width), F32),
            pltpu.VMEM((CHUNKS, side - 1, side, side * rows * halves, LANES), F32),
            pltpu.VMEM((CHUNKS, parts * GROUP, width), F32),
            pltpu.VMEM((CHUNKS, parts * GROUP * halves, LANES), F32),
            pltpu.VMEM((CHUNKS, chans * halves, LANES), F32),
            pltpu.VMEM((chans * halves, LANES), F32),
            pltpu.VMEM((CHUNKS, side, side, side) + block, F32),
            pltpu.VMEM((CHUNKS, side - 1, side, side) + block, F32),
            pltpu.VMEM((CHUNKS, side, side, side) + block, F32),
            pltpu.SemaphoreType.DMA((10,)),
            pltpu.SemaphoreType.DMA((34,)),
            pltpu.SemaphoreType.DMA((34,)),
        ],
        compiler_params=pltpu.CompilerParams(
            collective_id=0, has_side_effects=True, vmem_limit_bytes=44 * 2**20
        ),
        name="exchange",
    )(*[
        pltpu.with_memory_space_constraint(x, pltpu.HBM)
        for x in (
            domain_counts, token_ids[None, :], domain_ids[None, :], skip_gain, table,
            embed_table, query_act, key_act, conv_saved, loss_seed,
            filters.reshape(side, side, side, CHUNKS, GROUP, width),
        )
    ])
    return pl.pallas_call(
        write_out,
        out_shape=(hold,) * 4,
        in_specs=[pl.BlockSpec(memory_space=pl.ANY)] * 4,
        out_specs=(hbm,) * 4,
        scratch_shapes=[pltpu.SemaphoreType.DMA((4,))],
        compiler_params=pltpu.CompilerParams(vmem_limit_bytes=4 * 2**20),
        name="write_out",
    )(*[pltpu.with_memory_space_constraint(x, pltpu.VMEM) for x in results])


def write_out(*refs):
    semaphores = refs[-1]
    copies = [
        pltpu.make_async_copy(refs[i], refs[4 + i], semaphores.at[i]) for i in range(4)
    ]
    for copy in copies:
        copy.start()
    for copy in copies:
        copy.wait()


def solution(mesh):
    in_specs = (
        P("ctx"), P("ctx"), P("ctx", None), P(None, "chan"),
        P("chan", "ctx"), P("chan", "ctx"), P("chan", "ctx"), P("chan", "ctx"), P("chan", "ctx"),
        P("chan"),
    )
    out_specs = (P("chan", "ctx"),) * 4
    return jax.shard_map(
        on_device, mesh=mesh, in_specs=in_specs, out_specs=out_specs, check_vma=False
    )
```

```python
import functools

import jax
import jax.numpy as jnp
import ml_dtypes
import numpy as np
from jax import lax
from jax.experimental import pallas as pl
from jax.experimental.pallas import tpu as pltpu
from jax.sharding import PartitionSpec as P

MESH = pl.DeviceIdType.MESH
F32, BF16 = jnp.float32, jnp.bfloat16
count_unit = 64.0
LANES = 128
GROUP = 8
CHUNKS = 2
BATCH = 4


def split_host(x):
    high = x.astype(np.float32).astype(ml_dtypes.bfloat16)
    low = (x - high.astype(np.float64)).astype(np.float32).astype(ml_dtypes.bfloat16)
    return high, low


def constants(parts, width):
    total = parts * width
    j, r = np.arange(parts), np.arange(width)
    theta = 2.0 * np.pi * np.outer(j + 0.25, j) / parts
    first = np.concatenate([np.cos(theta), -np.sin(theta)], 0)
    phase = 2.0 * np.pi * np.outer(j + 0.25, r) / total
    omega = 2.0 * np.pi * (np.outer(r, r) % width) / width
    cosine, sine = np.cos(omega), np.sin(omega)
    inner = np.block([[cosine, -sine], [sine, cosine]])
    last = np.concatenate([np.cos(theta).T, np.sin(theta).T], 1) / total
    fh, fl = split_host(first)
    lh, ll = split_host(last)
    first_cat = np.concatenate([fh, fh, fl], 1)
    last_cat = np.concatenate([lh, lh, ll], 1)
    table = np.zeros((2 * width + 4 * parts, 2 * width), np.float32)
    table[: 2 * width] = inner
    table[2 * width : 2 * width + parts] = np.concatenate([np.cos(phase), np.sin(phase)], 1)
    table[2 * width + parts : 2 * width + 3 * parts, : 3 * parts] = first_cat
    table[2 * width + 3 * parts :, : 6 * parts] = last_cat
    return table


def split(x):
    high = x.astype(BF16)
    return high, (x - high.astype(F32)).astype(BF16)


def dot(a, b):
    return jnp.dot(a, b, preferred_element_type=F32)


def turned(a, b, cosine, sine):
    return a * cosine + b * sine, b * cosine - a * sine


def kernel(
    parts, width, side,
    counts, tokens, domains, skip, table,
    embed, query, key, saved, loss, filters,
    grad_query, grad_key, grad_value, grad_filter,
    counts_v, tokens_v, domains_v, skip_s, table_v,
    cnt_src, cnt_z, cnt_part, cnt_all,
    embed_v, query_v, key_v, saved_v, loss_v, first, last, inner_v, values_v, keyed_v,
    md, zf, zmd, rf, rfh, rmd, res_h, res, zres, out,
    load_sem, send_sem, recv_sem,
):
    me = lax.axis_index("ctx")
    chan = lax.axis_index("chan")
    x, z, y = me // (side * side), lax.rem(me // side, side), lax.rem(me, side)
    plane = side * side
    rows = CHUNKS * GROUP
    halves = width // LANES
    tall = rows * halves
    steps = (1, 2, 3)
    barrier = pltpu.get_barrier_semaphore()

    def along(k):
        return lax.rem(z + k, side)

    def z_peer(k):
        return (x * plane + along(k) * side + y, chan)

    def beside(i):
        return lax.rem(x + i // side, side), lax.rem(y + i, side)

    def xy_peer(i):
        xx, yy = beside(i)
        return (xx * plane + z * side + yy, chan)

    fetch = pltpu.make_async_copy(counts, counts_v, load_sem.at[9])
    fetch.start()

    def greet(i, carry):
        pl.semaphore_signal(barrier, inc=1, device_id=xy_peer(i), device_id_type=MESH)
        return carry

    for k in steps:
        pl.semaphore_signal(barrier, inc=1, device_id=z_peer(k), device_id_type=MESH)
    lax.fori_loop(1, plane, greet, 0)

    domain_count = counts.shape[1]
    cnt_src[...] = jnp.zeros_like(cnt_src)
    fetch.wait()
    cnt_src[0:1, 0:domain_count] = counts_v[...].astype(F32)

    def remote(source, target, slot, peer):
        pltpu.make_async_remote_copy(
            src_ref=source, dst_ref=target, send_sem=send_sem.at[slot], recv_sem=recv_sem.at[slot],
            device_id=peer, device_id_type=MESH,
        ).start()

    def spread_plane(source, target, slot):
        pltpu.make_async_copy(source(x, y), target, recv_sem.at[slot]).start()

        def go(i, carry):
            remote(source(*beside(i)), target, slot, xy_peer(i))
            return carry

        lax.fori_loop(1, plane, go, 0)

    def taken(like, slot, sem):
        pltpu.make_async_copy(like, like, sem.at[slot]).wait()

    def piece_of(ref, index, size):
        return ref.at[pl.ds(pl.multiple_of(index * size, size), size)]

    def source_index(k):
        return x * plane + lax.rem(z + side - k, side) * side + y

    cnt_slot, f_slot, md_slot, res_slot, end_slot = 0, (2, 22), (6, 10), (14, 17), (26, 27)

    pl.semaphore_wait(barrier, plane - 1 + side - 1)

    for k in steps:
        remote(cnt_src, cnt_z.at[k - 1], cnt_slot, z_peer(k))

    def send_filters(chunk):
        for k in steps:
            remote(
                filters.at[:, along(k), :, chunk], zf.at[chunk, k - 1], f_slot[chunk] + k, z_peer(k)
            )

    def send_filters_plane(chunk):
        spread_plane(
            lambda xx, yy: filters.at[xx, z, yy, chunk],
            piece_of(rf.at[chunk], source_index(0), GROUP),
            f_slot[chunk],
        )

    def forward_filters(chunk, k):
        taken(zf.at[chunk, k - 1], f_slot[chunk] + k, recv_sem)
        spread_plane(
            lambda xx, yy: zf.at[chunk, k - 1, xx, yy],
            piece_of(rf.at[chunk], source_index(k), GROUP),
            f_slot[chunk],
        )

    send_filters(0)
    loads = [
        pltpu.make_async_copy(source, target, load_sem.at[i])
        for i, (source, target) in enumerate(
            [
                (tokens, tokens_v), (domains, domains_v), (embed, embed_v), (key, key_v),
                (query, query_v), (saved, saved_v), (loss, loss_v), (skip, skip_s),
                (table, table_v),
            ]
        )
    ]
    for load in loads:
        load.start()
    send_filters_plane(0)

    for load in loads[0:3]:
        load.wait()
    vocab = embed_v.shape[0]
    onehot = (
        lax.broadcasted_iota(jnp.int32, (vocab, width), 0) == tokens_v[...]
    ).astype(F32).astype(BF16)
    piece = 128

    def look_up(b, carry):
        at = pl.multiple_of(b * piece, piece)
        values_v[pl.ds(at, piece), :] = lax.dot_general(
            embed_v[:, pl.ds(at, piece)], onehot, (((0,), (0,)), ((), ())),
            preferred_element_type=F32,
        )
        return carry

    taken(cnt_z, cnt_slot, recv_sem)
    cnt_part[...] = cnt_src[...] + cnt_z[0] + cnt_z[1] + cnt_z[2]
    spread_plane(lambda xx, yy: cnt_part, cnt_all.at[x * side + y], cnt_slot + 1)
    lax.fori_loop(0, values_v.shape[0] // piece, look_up, 0)
    for load in loads[3:7]:
        load.wait()
    taken(cnt_all, cnt_slot + 1, recv_sem)
    totals = jnp.sum(cnt_all[...], axis=0)
    shares = (count_unit * parts) / totals
    weight = jnp.zeros((1, width), F32)
    for d in range(domain_count):
        weight = jnp.where(domains_v[...] == d, shares[0:1, d : d + 1], weight)

    def products(b, carry):
        at = pl.multiple_of(b * piece, piece)
        block = pl.ds(at, piece)
        keyed = key_v[block, :].astype(F32)
        keyed_v[block, :] = keyed
        mixed = keyed * values_v[block, :]
        upstream = (loss_v[block, :].astype(F32) * weight).astype(BF16).astype(F32)
        grad_query[block, :] = upstream * saved_v[block, :].astype(F32)
        dconv = upstream * query_v[block, :].astype(F32)
        for q in range(piece // rows):
            owner = b * (piece // rows) + q
            ox, oz, oy = owner // plane, lax.rem(owner // side, side), q % side
            for chunk in range(CHUNKS):
                part = slice(q * rows + chunk * GROUP, q * rows + (chunk + 1) * GROUP)
                for h in range(halves):
                    start = oy * tall + h * GROUP
                    lanes = slice(h * LANES, (h + 1) * LANES)
                    md[chunk, ox, oz, start : start + GROUP, :] = mixed[part, lanes]
                    start = start + halves * GROUP
                    md[chunk, ox, oz, start : start + GROUP, :] = dconv[part, lanes]
        return carry

    lax.fori_loop(0, values_v.shape[0] // piece, products, 0)

    def send_signals(chunk):
        for k in steps:
            remote(md.at[chunk, :, along(k)], zmd.at[chunk, k - 1], md_slot[chunk] + k, z_peer(k))
        spread_plane(
            lambda xx, yy: piece_of(md.at[chunk, xx, z], yy, tall),
            piece_of(rmd.at[chunk], source_index(0), tall),
            md_slot[chunk],
        )

    def forward_signals(chunk, k):
        taken(zmd.at[chunk, k - 1], md_slot[chunk] + k, recv_sem)
        spread_plane(
            lambda xx, yy: piece_of(zmd.at[chunk, k - 1, xx], yy, tall),
            piece_of(rmd.at[chunk], source_index(k), tall),
            md_slot[chunk],
        )

    send_signals(0)
    for k in steps:
        forward_filters(0, k)

    for load in loads[7:]:
        load.wait()
    double = 2 * width
    first[...] = table_v[double + parts : double + 3 * parts, 0 : 3 * parts].astype(BF16)
    last[...] = table_v[double + 3 * parts : double + 4 * parts, 0 : 6 * parts].astype(BF16)
    inner_v[0], inner_v[1] = split(table_v[0:double, :])
    for k in steps:
        forward_signals(0, k)
        if k == steps[1]:
            send_filters(1)
            send_filters_plane(1)
    send_signals(1)

    def halve(chunk, b, carry):
        at = pl.multiple_of(b * piece, piece)
        block = rf[chunk, pl.ds(at, piece), :]
        for q in range(piece // GROUP):
            for h in range(halves):
                start = pl.multiple_of((at + q * GROUP) * halves + h * GROUP, GROUP)
                rfh[chunk, pl.ds(start, GROUP), :] = block[
                    q * GROUP : (q + 1) * GROUP, h * LANES : (h + 1) * LANES
                ]
        return carry

    def column(ref, start, stride):
        return jnp.concatenate(
            [ref[pl.ds(start + h * GROUP, parts, stride=stride), :] for h in range(halves)], axis=1
        )

    def inner_transform(real, imag):
        high, low = split(jnp.concatenate([real, imag], axis=1))
        count = high.shape[0]
        coarse = dot(jnp.concatenate([high, low], axis=0), inner_v[0])
        return coarse[:count] + coarse[count:] + dot(high, inner_v[1])

    def channels(chunk, g, carry):
        cosine = table_v[double : double + parts, 0:width]
        sine = table_v[double : double + parts, width:double]
        lines = [[], [], []]
        for p in range(BATCH):
            c = g * BATCH + p
            lines[0].append(column(rfh.at[chunk], c, GROUP * halves))
            lines[1].append(column(rmd.at[chunk], c, tall))
            lines[2].append(column(rmd.at[chunk], GROUP * halves + c, tall))
        turns = [[], [], []]
        for p in range(BATCH):
            high, low = split(jnp.concatenate([line[p] for line in lines], axis=1))
            spread = dot(first[...], jnp.concatenate([high, low, high], axis=0))
            for s in range(3):
                turns[s].append(
                    turned(
                        spread[:parts, s * width : (s + 1) * width],
                        spread[parts:, s * width : (s + 1) * width],
                        cosine, sine,
                    )
                )
        flat = turns[0] + turns[1] + turns[2]
        spectra = inner_transform(
            jnp.concatenate([t[0] for t in flat], axis=0),
            jnp.concatenate([t[1] for t in flat], axis=0),
        )
        real, imag = spectra[:, :width], spectra[:, width:]
        batch = BATCH * parts
        sr, si = real[2 * batch :], imag[2 * batch :]
        both_r = [real[s * batch : (s + 1) * batch] * sr + imag[s * batch : (s + 1) * batch] * si for s in (0, 1)]
        both_i = [imag[s * batch : (s + 1) * batch] * sr - real[s * batch : (s + 1) * batch] * si for s in (0, 1)]
        back = inner_transform(jnp.concatenate(both_r, axis=0), jnp.concatenate(both_i, axis=0))
        for p in range(BATCH):
            pairs = []
            for s in (0, 1):
                at = s * batch + p * parts
                pairs.append(turned(back[at : at + parts, :width], back[at : at + parts, width:], cosine, sine))
            folded = jnp.concatenate(
                [jnp.concatenate([t[0] for t in pairs], axis=1), jnp.concatenate([t[1] for t in pairs], axis=1)],
                axis=0,
            )
            high, low = split(folded)
            result = dot(last[...], jnp.concatenate([high, low, high], axis=0))
            c = g * BATCH + p
            gain = skip_s[me * rows + chunk * GROUP + c]
            both = (result[:, :width] + gain * lines[2][p], result[:, width:])
            for s in range(2):
                for h in range(halves):
                    start = (s * halves + h) * GROUP + c
                    res_h[pl.ds(start, parts, stride=tall), :] = both[s][
                        :, h * LANES : (h + 1) * LANES
                    ]
        return carry

    def widen(chunk, zz, xx, carry):
        for yy in range(side):
            start = pl.multiple_of((xx * plane + zz * side + yy) * tall, tall)
            for s in range(2):
                res[chunk, xx, zz, yy, s] = jnp.concatenate(
                    [
                        res_h[pl.ds(start + (s * halves + h) * GROUP, GROUP), :]
                        for h in range(halves)
                    ],
                    axis=1,
                )
        return carry

    def finish(chunk, oz, ox, carry):
        for q in range(side):
            here = pl.ds(
                pl.multiple_of(((ox * side + oz) * side + q) * rows + chunk * GROUP, GROUP), GROUP
            )
            back = out[chunk, ox, oz, q, 0]
            grad_key[here, :] = back * values_v[here, :]
            grad_value[here, :] = back * keyed_v[here, :]
            grad_filter[here, :] = out[chunk, ox, oz, q, 1] * ((parts * width) ** -0.5)
        return carry

    def transform(chunk):
        taken(rf.at[chunk], f_slot[chunk], recv_sem)
        lax.fori_loop(0, rf.shape[1] // piece, functools.partial(halve, chunk), 0)
        taken(rmd.at[chunk], md_slot[chunk], recv_sem)
        lax.fori_loop(0, GROUP // BATCH, functools.partial(channels, chunk), 0)
        for k in steps + (0,):
            zz = along(k)
            lax.fori_loop(0, side, functools.partial(widen, chunk, zz), 0)
            spread_plane(
                lambda xx, yy: res.at[chunk, xx, zz, yy],
                zres.at[chunk, k - 1, x, y] if k else out.at[chunk, x, z, y],
                res_slot[chunk] + k - 1 if k else end_slot[chunk],
            )

    def forward_results(chunk, k):
        taken(zres.at[chunk, k - 1], res_slot[chunk] + k - 1, recv_sem)
        remote(zres.at[chunk, k - 1], out.at[chunk, :, z], end_slot[chunk] + 2 * k, z_peer(k))

    transform(0)
    for k in steps:
        forward_filters(1, k)
    for k in steps:
        forward_signals(1, k)
        forward_results(0, k)
    transform(1)
    for k in steps:
        forward_results(1, k)

    taken(cnt_z, cnt_slot, send_sem)
    taken(cnt_all.at[pl.ds(0, plane - 1)], cnt_slot + 1, send_sem)
    for chunk in range(CHUNKS):
        for k in steps:
            taken(zf.at[chunk, k - 1], f_slot[chunk] + k, send_sem)
            taken(zmd.at[chunk, k - 1], md_slot[chunk] + k, send_sem)
            taken(rmd.at[chunk, pl.ds(0, (plane - 1) * tall)], res_slot[chunk] + k - 1, send_sem)
        taken(rf.at[chunk, pl.ds(0, (parts - side) * GROUP)], f_slot[chunk], send_sem)
        taken(rmd.at[chunk, pl.ds(0, (parts - side) * tall)], md_slot[chunk], send_sem)
    for chunk in range(CHUNKS):
        for k in (0,) + steps:
            oz = lax.rem(z + side - k, side)
            taken(out.at[chunk, :, oz], end_slot[chunk] + 2 * k, recv_sem)
            lax.fori_loop(0, side, functools.partial(finish, chunk, oz), 0)
    for chunk in range(CHUNKS):
        taken(rmd.at[chunk, pl.ds(0, (plane - 1) * tall)], end_slot[chunk], send_sem)
        for k in steps:
            taken(zres.at[chunk, k - 1], end_slot[chunk] + 2 * k, send_sem)


def on_device(
    token_ids, domain_ids, domain_counts, embed_table, query_act, key_act, conv_saved,
    loss_seed, filters, skip_gain,
):
    parts = lax.axis_size("ctx")
    chans, width = query_act.shape
    vocab = embed_table.shape[0]
    table = jnp.asarray(constants(parts, width))
    vmem = pl.BlockSpec(memory_space=pltpu.VMEM)
    hbm = pl.BlockSpec(memory_space=pltpu.HBM)
    rows = CHUNKS * GROUP
    halves = width // LANES
    side = 4
    assert chans == parts * rows and parts == side**3
    block = (2, GROUP, width)
    hold = jax.ShapeDtypeStruct((chans, width), F32)
    results = pl.pallas_call(
        functools.partial(kernel, parts, width, side),
        out_shape=(hold,) * 4,
        in_specs=[hbm] * 11,
        out_specs=(vmem,) * 4,
        scratch_shapes=[
            pltpu.VMEM(domain_counts.shape, jnp.int32),
            pltpu.VMEM((1, width), jnp.int32),
            pltpu.VMEM((1, width), jnp.int32),
            pltpu.SMEM((chans,), F32),
            pltpu.VMEM(table.shape, F32),
            pltpu.VMEM((1, LANES), F32),
            pltpu.VMEM((side - 1, 1, LANES), F32),
            pltpu.VMEM((1, LANES), F32),
            pltpu.VMEM((side**2, 1, LANES), F32),
            pltpu.VMEM((vocab, chans), BF16),
            pltpu.VMEM((chans, width), BF16),
            pltpu.VMEM((chans, width), BF16),
            pltpu.VMEM((chans, width), BF16),
            pltpu.VMEM((chans, width), BF16),
            pltpu.VMEM((2 * parts, 3 * parts), BF16),
            pltpu.VMEM((parts, 6 * parts), BF16),
            pltpu.VMEM((2, 2 * width, 2 * width), BF16),
            pltpu.VMEM((chans, width), F32),
            pltpu.VMEM((chans, width), F32),
            pltpu.VMEM((CHUNKS, side, side, side * rows * halves, LANES), F32),
            pltpu.VMEM((CHUNKS, side - 1, side, side, GROUP, width), F32),
            pltpu.VMEM((CHUNKS, side - 1, side, side * rows * halves, LANES), F32),
            pltpu.VMEM((CHUNKS, parts * GROUP, width), F32),
            pltpu.VMEM((CHUNKS, parts * GROUP * halves, LANES), F32),
            pltpu.VMEM((CHUNKS, chans * halves, LANES), F32),
            pltpu.VMEM((chans * halves, LANES), F32),
            pltpu.VMEM((CHUNKS, side, side, side) + block, F32),
            pltpu.VMEM((CHUNKS, side - 1, side, side) + block, F32),
            pltpu.VMEM((CHUNKS, side, side, side) + block, F32),
            pltpu.SemaphoreType.DMA((10,)),
            pltpu.SemaphoreType.DMA((34,)),
            pltpu.SemaphoreType.DMA((34,)),
        ],
        compiler_params=pltpu.CompilerParams(
            collective_id=0, has_side_effects=True, vmem_limit_bytes=44 * 2**20
        ),
        name="exchange",
    )(*[
        pltpu.with_memory_space_constraint(x, pltpu.HBM)
        for x in (
            domain_counts, token_ids[None, :], domain_ids[None, :], skip_gain, table,
            embed_table, query_act, key_act, conv_saved, loss_seed,
            filters.reshape(side, side, side, CHUNKS, GROUP, width),
        )
    ])
    return pl.pallas_call(
        write_out,
        out_shape=(hold,) * 4,
        in_specs=[pl.BlockSpec(memory_space=pl.ANY)] * 4,
        out_specs=(hbm,) * 4,
        scratch_shapes=[pltpu.SemaphoreType.DMA((4,))],
        compiler_params=pltpu.CompilerParams(vmem_limit_bytes=4 * 2**20),
        name="write_out",
    )(*[pltpu.with_memory_space_constraint(x, pltpu.VMEM) for x in results])


def write_out(*refs):
    semaphores = refs[-1]
    copies = [
        pltpu.make_async_copy(refs[i], refs[4 + i], semaphores.at[i]) for i in range(4)
    ]
    for copy in copies:
        copy.start()
    for copy in copies:
        copy.wait()


def solution(mesh):
    in_specs = (
        P("ctx"), P("ctx"), P("ctx", None), P(None, "chan"),
        P("chan", "ctx"), P("chan", "ctx"), P("chan", "ctx"), P("chan", "ctx"), P("chan", "ctx"),
        P("chan"),
    )
    out_specs = (P("chan", "ctx"),) * 4
    return jax.shard_map(
        on_device, mesh=mesh, in_specs=in_specs, out_specs=out_specs, check_vma=False
    )
```
